512 devices in a mesh: pipe: 8 (over y_lo, core), ctx: 32 (over x, z), dp: 2 (over y_hi).
Axes of the slice: x: 4, y: 8 (y_hi: 2, y_lo: 4; y = y_hi * 4 + y_lo), z: 8, core: 2. Of those that a mesh axis runs over, the one named last changes fastest.
Arguments:
- section_queries: bfloat16 [8, 8192, 4096], P('pipe', ('ctx', 'dp')), may hold values from -20 to 20
- section_keys: bfloat16 [8, 8192, 512], P('pipe', ('ctx', 'dp')), may hold values from -20 to 20
- cascade_value_rows: bfloat16 [8, 8192, 512], P('pipe', ('ctx', 'dp')), may hold values from -6 to 6
- output_grad: bfloat16 [8, 8192, 4096], P('pipe', ('ctx', 'dp')), may hold values from -6 to 6
- segments: int32 [8192], replicated, may hold values from 0 to 53, never falling along the last dimension, each value on 1 to 448 neighbouring positions
- stretch_plan: int32 [128], replicated, may hold values from 0 to 127, as said below
Outputs:
- section_output: bfloat16 [8, 8192, 4096], P('pipe', ('ctx', 'dp'))
- query_grad_sent: bfloat16 [8, 8192, 4096], P('pipe', ('ctx', 'dp'))
- key_grad: bfloat16 [8, 8192, 512], P('pipe', ('ctx', 'dp'))
- value_grad: bfloat16 [8, 8192, 512], P('pipe', ('ctx', 'dp'))
The draws below stay inside these ranges and needn't reach their ends.
Inputs may be any that keep to these rules, and one draw needn't show every extreme that they name: `stretch_plan`: A permutation of the 128 half-blocks. Slots 2 * i and 2 * i + 1 belong to index i of ctx+dp; each holds one of that index's own two half-blocks or the half-block of a neighbouring index that adjoins index i's tokens.
All inputs are finite; a program needn't handle non-finite values.
Results may differ from the reference program's by a relative error of at most 0.012.
The reference program's roundings to bfloat16 on the way (of `probs_low`, `attended`, `grad_scores` and `query_grad`) count: a program that leaves them out, or rounds other values in their place, can miss the bound.
Values may be sent and summed in bfloat16 or wider, within the bound.
A program may use at most 64 MiB of HBM per device.

```python
import math
import jax
import jax.numpy as jnp
import numpy as np
from jax import lax

QUERY_HEADS = 32
KEY_VALUE_HEADS = 4
HEAD_SIZE = 128
TOK_DEV = 128
PACKED_TOKENS = 8192
CASCADE_PARTS = 8
SLOTS = 128
DOCLEN = 448
DOCS = 54


def draw_section_queries(key, part):
    key = jax.random.fold_in(key, 3)
    value_rows = jnp.clip(jax.random.normal(key, (CASCADE_PARTS, PACKED_TOKENS, QUERY_HEADS * HEAD_SIZE), jnp.float32), -6.0, 6.0)
    return value_rows.astype(jnp.bfloat16)


def draw_section_keys(key, part):
    key = jax.random.fold_in(key, 7)
    value_rows = jnp.clip(jax.random.normal(key, (CASCADE_PARTS, PACKED_TOKENS, KEY_VALUE_HEADS * HEAD_SIZE), jnp.float32), -6.0, 6.0)
    return value_rows.astype(jnp.bfloat16)


def draw_stretch_plan(key, part):
    key = jax.random.fold_in(key, 5)
    holders = SLOTS // 2
    index_rows = jnp.arange(holders, dtype=jnp.int32)
    lower_piece = jnp.where(index_rows == 0, 0, 2 * index_rows - 1)
    upper_piece = jnp.where(index_rows == holders - 1, SLOTS - 1, 2 * index_rows + 2)
    flips = jax.random.randint(key, (holders,), 0, 2)
    first_slot = jnp.where(flips == 1, upper_piece, lower_piece)
    second_slot = jnp.where(flips == 1, lower_piece, upper_piece)
    return jnp.stack([first_slot, second_slot], axis=1).reshape(SLOTS).astype(jnp.int32)


def steps_of(stream_key, shape, cuts, smallest, top_value):
    def one(dim, shards_of):
        steps = jax.random.uniform(jax.random.fold_in(jax.random.fold_in(stream_key, 6), dim), (shards_of,), jnp.float32, smallest / len(cuts), top_value / len(cuts))
        return jnp.repeat(jnp.exp(steps), shape[dim] // shards_of).reshape((-1,) + (1,) * (len(shape) - dim - 1))

    gain = one(*cuts[0])
    for cut in cuts[1:]:
        gain = gain * one(*cut)
    return gain


def split_up(count, total, most, lean):
    weights = [(1 << 20) // math.isqrt(standing ** lean) + 1 for standing in range(2, count + 1)]
    surplus, given = total - most - (count - 1), [1] * (count - 1)
    while surplus > 0:
        movable = [i for i in range(count - 1) if given[i] < most]
        whole, budget = sum([weights[i] for i in movable]), surplus
        for i in movable:
            addition = min(most - given[i], max(1, budget * weights[i] // whole), surplus)
            given[i] = given[i] + addition
            surplus = surplus - addition
    return np.array([most] + given)


def ragged(key, count, total, limit, lean):
    if count == 2:
        one = jax.random.randint(key, (), max(1, total - limit), min(limit, total - 1) + 1)
        return jnp.stack([one, total - one])
    sizes = jnp.asarray(split_up(count, total, limit, lean), jnp.int32)
    pairs = (count - 1) // 2
    source_of, receiver = sizes[1:1 + 2 * pairs:2], sizes[2:2 + 2 * pairs:2]
    room = jnp.minimum(source_of - 1, limit - receiver)
    shifted = jax.random.randint(jax.random.fold_in(key, 1), (pairs,), 0, 1 << 20) % (room + 1)
    sizes = sizes.at[1:1 + 2 * pairs:2].set(source_of - shifted).at[2:2 + 2 * pairs:2].set(receiver + shifted)
    return sizes[jax.random.permutation(jax.random.fold_in(key, 2), count)]


def bell_draw(rng, extent, deviation, most, shards=(), kind=jnp.bfloat16):
    drawn = deviation * jax.random.normal(rng, extent, jnp.float32)
    if shards:
        drawn = drawn * steps_of(rng, extent, shards, -0.22, 0.18)
    return jnp.clip(drawn, -most, most).astype(kind)


def setup_inputs(seed: int = 0) -> dict:
    key_list = jax.random.split(jax.random.key(seed), 7)
    return {
        "section_queries": draw_section_queries(jax.random.fold_in(key_list[6], 71), 0),
        "section_keys": draw_section_keys(jax.random.fold_in(key_list[6], 71), 0),
        "cascade_value_rows": bell_draw(key_list[2], (CASCADE_PARTS, PACKED_TOKENS, KEY_VALUE_HEADS * HEAD_SIZE), 1.0, 6.0, ((0, 8), (1, 64))),
        "output_grad": bell_draw(key_list[3], (CASCADE_PARTS, PACKED_TOKENS, QUERY_HEADS * HEAD_SIZE), 1.0, 6.0, ((0, 8), (1, 64))),
        "segments": jnp.searchsorted(jnp.cumsum(ragged(key_list[4], DOCS, PACKED_TOKENS, DOCLEN, 2)), jnp.arange(PACKED_TOKENS), side="right").astype(jnp.int32),
        "stretch_plan": draw_stretch_plan(jax.random.fold_in(key_list[6], 71), 0),
    }


def rounded(value):
    return lax.optimization_barrier(value.astype(jnp.bfloat16)).astype(jnp.float32)

def one_section(arrays, segments, stretch_plan):
    query_rows, keys_in, values_in, incoming_gradient = arrays
    head_groupings = QUERY_HEADS // KEY_VALUE_HEADS
    half_block_rows = TOK_DEV // 2
    window_extent = DOCLEN - 1 + half_block_rows
    scaling = 1.0 / math.sqrt(HEAD_SIZE)
    key_padding = jnp.pad(keys_in.astype(jnp.float32), ((window_extent, 0), (0, 0)))
    value_padding = jnp.pad(values_in.astype(jnp.float32), ((window_extent, 0), (0, 0)))
    seg_pad = jnp.pad(segments, (window_extent, 0), constant_values=-1)
    offsets = jnp.arange(half_block_rows, dtype=jnp.int32)
    spans = jnp.arange(window_extent, dtype=jnp.int32)

    def per_slot(carry, place_index):
        key_gradient_total, value_gradient_total = carry
        block = stretch_plan[place_index]
        begin_offset = (block * half_block_rows).astype(jnp.int32)
        query_block_rows = lax.dynamic_slice_in_dim(query_rows, begin_offset, half_block_rows, 0).astype(jnp.float32).reshape(half_block_rows, KEY_VALUE_HEADS, head_groupings, HEAD_SIZE)
        gradient_block_rows = lax.dynamic_slice_in_dim(incoming_gradient, (place_index * half_block_rows).astype(jnp.int32), half_block_rows, 0).astype(jnp.float32).reshape(half_block_rows, KEY_VALUE_HEADS, head_groupings, HEAD_SIZE)
        window_begin_offset = (begin_offset + half_block_rows).astype(jnp.int32)
        key_block_rows = lax.dynamic_slice_in_dim(key_padding, window_begin_offset, window_extent, 0).reshape(window_extent, KEY_VALUE_HEADS, HEAD_SIZE)
        value_block_rows = lax.dynamic_slice_in_dim(value_padding, window_begin_offset, window_extent, 0).reshape(window_extent, KEY_VALUE_HEADS, HEAD_SIZE)
        query_pos = begin_offset + offsets
        key_pos = begin_offset + half_block_rows - window_extent + spans
        query_seg = lax.dynamic_slice_in_dim(segments, begin_offset, half_block_rows)
        key_seg = lax.dynamic_slice_in_dim(seg_pad, window_begin_offset, window_extent)
        visible = (query_seg[:, None] == key_seg[None, :]) & (key_pos[None, :] <= query_pos[:, None])
        scores = jnp.einsum('igha,jga->ghij', query_block_rows, key_block_rows) * scaling
        scores = jnp.where(visible[None, None], scores, -jnp.inf)
        top = lax.optimization_barrier(jnp.max(scores, axis=-1, keepdims=True))
        weights = jnp.exp(scores - top)
        probs = weights / lax.optimization_barrier(jnp.sum(weights, axis=-1, keepdims=True))
        probs_low = rounded(probs)
        attended = rounded(jnp.einsum('ghij,jga->igha', probs_low, value_block_rows))
        grad_probs = jnp.einsum('igha,jga->ghij', gradient_block_rows, value_block_rows)
        delta = jnp.einsum('igha,igha->ghi', gradient_block_rows, attended)
        grad_scores = rounded(probs * (grad_probs - delta[..., None]))
        query_grad = jnp.einsum('ghij,jga->igha', grad_scores, key_block_rows) * scaling
        key_portion = jnp.einsum('ghij,igha->jga', grad_scores, query_block_rows) * scaling
        value_portion = jnp.einsum('ghij,igha->jga', probs_low, gradient_block_rows)
        prior_keys = lax.dynamic_slice_in_dim(key_gradient_total, window_begin_offset, window_extent, 0)
        key_gradient_total = lax.dynamic_update_slice_in_dim(key_gradient_total, prior_keys + key_portion.reshape(window_extent, KEY_VALUE_HEADS * HEAD_SIZE), window_begin_offset, 0)
        prior_values = lax.dynamic_slice_in_dim(value_gradient_total, window_begin_offset, window_extent, 0)
        value_gradient_total = lax.dynamic_update_slice_in_dim(value_gradient_total, prior_values + value_portion.reshape(window_extent, KEY_VALUE_HEADS * HEAD_SIZE), window_begin_offset, 0)
        results = (attended.reshape(half_block_rows, QUERY_HEADS * HEAD_SIZE).astype(jnp.bfloat16), query_grad.reshape(half_block_rows, QUERY_HEADS * HEAD_SIZE).astype(jnp.bfloat16))
        return ((key_gradient_total, value_gradient_total), results)
    empty_total = jnp.zeros((window_extent + PACKED_TOKENS, KEY_VALUE_HEADS * HEAD_SIZE), jnp.float32)
    slot_ids = jnp.arange(PACKED_TOKENS // half_block_rows, dtype=jnp.int32)
    (key_gradient_total, value_gradient_total), (attended, query_grad) = lax.scan(per_slot, (empty_total, empty_total), slot_ids)
    attended = attended.reshape(PACKED_TOKENS, QUERY_HEADS * HEAD_SIZE)
    query_grad = query_grad.reshape(PACKED_TOKENS, QUERY_HEADS * HEAD_SIZE)
    return (attended, query_grad, key_gradient_total[window_extent:].astype(jnp.bfloat16), value_gradient_total[window_extent:].astype(jnp.bfloat16))

def reference(section_queries, section_keys, cascade_value_rows, output_grad, segments, stretch_plan):

    def run_section(arrays):
        return one_section(arrays, segments, stretch_plan)
    attended, query_grad, key_grad, value_grad = lax.map(run_section, (section_queries, section_keys, cascade_value_rows, output_grad))
    empty_filler = jnp.zeros_like(attended[:1])
    section_output = jnp.concatenate([empty_filler, attended[:-1]], axis=0)
    query_grad_sent = jnp.concatenate([query_grad[1:], empty_filler], axis=0)
    return (section_output, query_grad_sent, key_grad, value_grad)
```

```python
import functools
import math

import jax
import jax.numpy as jnp
from jax import lax
from jax.experimental import pallas as pl
from jax.experimental.pallas import tpu as pltpu
from jax.sharding import PartitionSpec as P

QUERY_HEADS = 32
KEY_VALUE_HEADS = 4
HEAD_SIZE = 128
GROUP = QUERY_HEADS // KEY_VALUE_HEADS
MESH = pl.DeviceIdType.MESH
F32 = jnp.float32
BF16 = jnp.bfloat16
LOW = -1e30


def _nt(a, b):
    return lax.dot_general(a, b, (((1,), (1,)), ((), ())), preferred_element_type=F32)


def _nn(a, b):
    return lax.dot_general(a, b, (((1,), (0,)), ((), ())), preferred_element_type=F32)


def _tn(a, b):
    return lax.dot_general(a, b, (((0,), (0,)), ((), ())), preferred_element_type=F32)


def one_of(index, choices):
    first, second, third, fourth = choices
    return lax.select(
        index < 2, lax.select(index == 0, first, second), lax.select(index == 2, third, fourth)
    )


def _kernel(
    sizes,
    plan_ref,
    seg_ref,
    q_hbm,
    k_hbm,
    v_hbm,
    do_hbm,
    so_out,
    qg_out,
    kg_out,
    vg_out,
    kv,
    qb,
    dob,
    att,
    dqb,
    bias,
    parts,
    loc,
    ret,
    back,
    psend,
    precv,
    loc_sem,
    kv_send,
    kv_recv,
    q_send,
    q_recv,
    out_send,
    out_recv,
    ret_send,
    ret_recv,
    fin_send,
    fin_recv,
):
    n_pipe, n_ctx = sizes
    rows = k_hbm.shape[0]
    half = rows // 2
    width = GROUP * HEAD_SIZE
    window = 8 * half
    pad = 3 * half
    groups = KEY_VALUE_HEADS
    scale = 1.0 / math.sqrt(HEAD_SIZE)
    exp_scale = scale * math.log2(math.e)

    p = lax.axis_index("pipe")
    c = lax.axis_index("ctx")
    d = lax.axis_index("dp")
    me = 2 * c + d

    def at(dc, dd):
        return {"pipe": p, "ctx": lax.rem(c + dc + n_ctx, n_ctx), "dp": dd}

    other = at(0, 1 - d)
    across = at(2 * d - 1, 1 - d)
    above = at(d, 1 - d)
    below = at(d - 1, 1 - d)
    up1, up2, down1, down2 = at(1, d), at(2, d), at(-1, d), at(-2, d)
    later = {"pipe": lax.rem(p + 1, n_pipe), "ctx": c, "dp": d}
    earlier = {"pipe": lax.rem(p + n_pipe - 1, n_pipe), "ctx": c, "dp": d}

    def remote(src, dst, send, recv, target):
        return pltpu.make_async_remote_copy(
            src_ref=src, dst_ref=dst, send_sem=send, recv_sem=recv, device_id=target, device_id_type=MESH
        )

    own = pl.ds(4 * rows, rows)
    kv_width = k_hbm.shape[1]
    own_k = pltpu.make_async_copy(k_hbm, kv.at[own, pl.ds(0, kv_width)], loc_sem.at[0])
    own_v = pltpu.make_async_copy(v_hbm, kv.at[own, pl.ds(kv_width, kv_width)], loc_sem.at[1])

    def own_q(g):
        return pltpu.make_async_copy(
            q_hbm.at[:, pl.ds(pl.multiple_of(g * width, width), width)],
            qb.at[g, pl.ds(half, rows)],
            loc_sem.at[2 + g],
        )

    def own_do(g):
        return pltpu.make_async_copy(
            do_hbm.at[:, pl.ds(pl.multiple_of(g * width, width), width)], dob.at[g], loc_sem.at[2 + groups + g]
        )

    own_k.start()
    own_v.start()
    for g in range(groups):
        own_q(g).start()
    for g in range(groups):
        own_do(g).start()

    barrier = pltpu.get_barrier_semaphore()
    for target in (other, across, up1, up2, down1, down2):
        pl.semaphore_signal(barrier, inc=1, device_id=target, device_id_type=MESH)

    @pl.when(p < n_pipe - 1)
    def _():
        pl.semaphore_signal(barrier, inc=1, device_id=later, device_id_type=MESH)

    @pl.when(p > 0)
    def _():
        pl.semaphore_signal(barrier, inc=1, device_id=earlier, device_id_type=MESH)

    own_k.wait()
    own_v.wait()
    for g in range(groups):
        own_q(g).wait()
    pl.semaphore_wait(
        barrier, 6 + jnp.where(p < n_pipe - 1, 1, 0).astype(jnp.int32) + jnp.where(p > 0, 1, 0).astype(jnp.int32)
    )

    def kv_copy(kind, source, place, target):
        return remote(
            kv.at[pl.ds(pl.multiple_of(source * rows, rows), rows)],
            kv.at[pl.ds(pl.multiple_of(place * rows, rows), rows)],
            kv_send.at[kind],
            kv_recv.at[kind],
            target,
        )

    kv_other = kv_copy(0, 4, 3 + 2 * d, other)
    kv_up1 = kv_copy(1, 4, 2, up1)
    kv_up2 = kv_copy(2, 4, 0, up2)
    kv_pass1 = kv_copy(3, 5 - 2 * d, 3 - 2 * d, up1)
    kv_pass2 = kv_copy(4, 5 - 2 * d, 1 + 4 * d, at(2 - 3 * d, d))

    def q_below(g):
        return remote(
            qb.at[g, pl.ds(half, half)], qb.at[g, pl.ds(3 * half, half)], q_send.at[0, g], q_recv.at[0, g], below
        )

    def q_above(g):
        return remote(
            qb.at[g, pl.ds(2 * half, half)], qb.at[g, pl.ds(0, half)], q_send.at[1, g], q_recv.at[1, g], above
        )

    kv_other.start()
    kv_up1.start()
    kv_up2.start()
    for g in range(groups):
        q_below(g).start()
        q_above(g).start()

    zeros = jnp.zeros((pad, 2 * HEAD_SIZE), F32)
    shifts = []
    row_at = lax.broadcasted_iota(jnp.int32, seg_ref.shape, 0)
    for s in range(2):
        block = plan_ref[2 * me + s]
        shifts.append(block - 2 * me + 1)
        pair = lax.div(block, 2)
        line = jnp.sum(jnp.where(row_at == pair, seg_ref[...].astype(F32), 0.0), axis=0, keepdims=True)
        lane = lax.broadcasted_iota(jnp.int32, (half, rows), 1)
        sub = lax.broadcasted_iota(jnp.int32, (half, rows), 0)
        picked = jnp.where(lane == sub + (block - 2 * pair) * half, jnp.broadcast_to(line, (half, rows)), 0.0)
        mine = jnp.sum(picked, axis=1, keepdims=True)

        def count(r, total, mine=mine):
            row = seg_ref[pl.ds(r, 1), :].astype(F32)
            return total + jnp.where(row < mine, 1.0, 0.0)

        total = lax.fori_loop(0, seg_ref.shape[0], count, jnp.zeros((half, rows), F32))
        first = jnp.sum(total, axis=1, keepdims=True)
        key_at = lax.broadcasted_iota(jnp.int32, (half, window), 1) + (block - 7) * half
        query_at = lax.broadcasted_iota(jnp.int32, (half, window), 0) + block * half
        seen = (key_at.astype(F32) >= first) & (key_at <= query_at)
        bias[s] = jnp.where(seen, 0.0, LOW)
        parts[s, pl.ds(0, pad)] = zeros
        parts[s, pl.ds(pad + window, pad + rows - half)] = jnp.zeros((pad + rows - half, 2 * HEAD_SIZE), F32)

    kv_other.wait_recv()
    kv_pass1.start()
    kv_pass2.start()
    for copy in (kv_up1, kv_up2, kv_pass1, kv_pass2):
        copy.wait_recv()
    for g in range(groups):
        own_do(g).wait()

    def columns(g):
        return pl.ds(pl.multiple_of(g * width, width), width)

    def att_copy(g):
        return remote(att.at[g], so_out.at[:, columns(g)], out_send.at[0, g], out_recv.at[0, g], later)

    def dq_copy(g):
        return remote(dqb.at[g], qg_out.at[:, columns(g)], out_send.at[1, g], out_recv.at[1, g], earlier)

    def ret_copy(g, kind):
        source, target = ((0, down2), (2, down1), (3 - 2 * d, down1), (1 + 4 * d, at(3 * d - 2, d)))[kind]
        return remote(ret.at[g, source], back.at[g, kind], ret_send.at[g, kind], ret_recv.at[g, kind], target)

    def fin_copy(g):
        return remote(psend.at[g], precv.at[g], fin_send.at[g], fin_recv.at[g], other)

    def window_part(o):
        total = None
        for s in range(2):
            starts = [pl.multiple_of(pad - k * half + o * rows, half) for k in range(4)]
            one = one_of(shifts[s], [parts[s, pl.ds(start, rows), :] for start in starts])
            total = one if total is None else total + one
        return total

    def pass_on(g):
        for kind in range(4):
            ret_copy(g, kind).wait_recv()
        total = loc[g, 1] + back[g, 2].astype(F32) + back[g, 3].astype(F32)
        psend[g] = total.astype(BF16)
        fin_copy(g).start()

    def one_group(g, carry):
        q_below(g).wait_recv()
        q_above(g).wait_recv()
        for s in range(2):
            shift = shifts[s]
            chosen = one_of(shift, [qb[g, pl.ds(k * half, half), :] for k in range(4)])
            grad = dob[g, pl.ds(s * half, half), :]
            heads = [slice(h * HEAD_SIZE, (h + 1) * HEAD_SIZE) for h in range(GROUP)]
            qs = jnp.concatenate([chosen[:, h] for h in heads], axis=0)
            gs = jnp.concatenate([grad[:, h] for h in heads], axis=0)
            k_place = pl.ds(pl.multiple_of(g * HEAD_SIZE, HEAD_SIZE), HEAD_SIZE)
            v_place = pl.ds(pl.multiple_of(kv_width + g * HEAD_SIZE, HEAD_SIZE), HEAD_SIZE)
            ks = one_of(shift, [kv[pl.ds(k * half, window), k_place] for k in range(4)])
            vs = one_of(shift, [kv[pl.ds(k * half, window), v_place] for k in range(4)])
            scores = _nt(qs, ks).reshape(GROUP, half, window) + bias[s][None]
            scores = scores.reshape(GROUP * half, window)
            top = jnp.max(scores, axis=1, keepdims=True)
            weights = jnp.exp2((scores - top) * exp_scale)
            probs = weights * (1.0 / jnp.sum(weights, axis=1, keepdims=True))
            low = probs.astype(BF16)
            attended = _nn(low, vs).astype(BF16)
            grad_probs = _nt(gs, vs)
            delta = jnp.sum(gs.astype(F32) * attended.astype(F32), axis=1, keepdims=True)
            grad_scores = (probs * (grad_probs - delta)).astype(BF16)
            query_grad = (_nn(grad_scores, ks) * scale).astype(BF16)
            for h in range(GROUP):
                att[g, pl.ds(s * half, half), heads[h]] = attended[h * half : (h + 1) * half]
                dqb[g, pl.ds(s * half, half), heads[h]] = query_grad[h * half : (h + 1) * half]
            parts[s, pl.ds(pad, window), pl.ds(0, HEAD_SIZE)] = _tn(grad_scores, qs) * scale
            parts[s, pl.ds(pad, window), pl.ds(HEAD_SIZE, HEAD_SIZE)] = _tn(low, gs)
        for o in range(6):
            ret[g, o] = window_part(o).astype(BF16)
        loc[g, 0] = window_part(4)
        loc[g, 1] = window_part(5 - 2 * d)
        for kind in range(4):
            ret_copy(g, kind).start()

        @pl.when(p < n_pipe - 1)
        def _():
            att_copy(g).start()

        @pl.when(p > 0)
        def _():
            dq_copy(g).start()

        @pl.when(g > 0)
        def _():
            pass_on(g - 1)

        return carry

    lax.fori_loop(0, groups, one_group, 0)
    pass_on(groups - 1)

    def finish(g, carry):
        fin_copy(g).wait_recv()
        total = loc[g, 0] + back[g, 0].astype(F32) + back[g, 1].astype(F32) + precv[g].astype(F32)
        place = pl.ds(pl.multiple_of(g * HEAD_SIZE, HEAD_SIZE), HEAD_SIZE)
        kg_out[:, place] = total[:, :HEAD_SIZE].astype(BF16)
        vg_out[:, place] = total[:, HEAD_SIZE:].astype(BF16)
        return carry

    lax.fori_loop(0, groups, finish, 0)

    for copy in (kv_other, kv_up1, kv_up2, kv_pass1, kv_pass2):
        copy.wait_send()

    def drain(g, carry):
        q_below(g).wait_send()
        q_above(g).wait_send()
        for kind in range(4):
            ret_copy(g, kind).wait_send()
        fin_copy(g).wait_send()

        @pl.when(p < n_pipe - 1)
        def _():
            att_copy(g).wait_send()
            dq_copy(g).wait_recv()

        @pl.when(p > 0)
        def _():
            dq_copy(g).wait_send()
            att_copy(g).wait_recv()

        return carry

    lax.fori_loop(0, groups, drain, 0)


def _on_device(sizes, section_queries, section_keys, cascade_value_rows, output_grad, segments, stretch_plan):
    _, rows, width = section_queries.shape
    kv_width = section_keys.shape[2]
    groups, half = KEY_VALUE_HEADS, rows // 2
    share = width // groups
    hbm = pl.BlockSpec(memory_space=pl.ANY)
    vmem = pl.BlockSpec(memory_space=pltpu.VMEM)
    dma = pltpu.SemaphoreType.DMA
    attended, query_grad, key_grad, value_grad = pl.pallas_call(
        functools.partial(_kernel, sizes),
        out_shape=[
            jax.ShapeDtypeStruct((rows, width), BF16),
            jax.ShapeDtypeStruct((rows, width), BF16),
            jax.ShapeDtypeStruct((rows, kv_width), BF16),
            jax.ShapeDtypeStruct((rows, kv_width), BF16),
        ],
        in_specs=[pl.BlockSpec(memory_space=pltpu.SMEM), vmem, hbm, hbm, hbm, hbm],
        out_specs=[hbm, hbm, vmem, vmem],
        scratch_shapes=[
            pltpu.VMEM((6 * rows, 2 * kv_width), BF16),
            pltpu.VMEM((groups, 2 * rows, share), BF16),
            pltpu.VMEM((groups, rows, share), BF16),
            pltpu.VMEM((groups, rows, share), BF16),
            pltpu.VMEM((groups, rows, share), BF16),
            pltpu.VMEM((2, half, 8 * half), F32),
            pltpu.VMEM((2, 14 * half + rows // 2, 2 * HEAD_SIZE), F32),
            pltpu.VMEM((groups, 2, rows, 2 * HEAD_SIZE), F32),
            pltpu.VMEM((groups, 6, rows, 2 * HEAD_SIZE), BF16),
            pltpu.VMEM((groups, 4, rows, 2 * HEAD_SIZE), BF16),
            pltpu.VMEM((groups, rows, 2 * HEAD_SIZE), BF16),
            pltpu.VMEM((groups, rows, 2 * HEAD_SIZE), BF16),
            dma((2 + 2 * groups,)),
            dma((5,)),
            dma((5,)),
            dma((2, groups)),
            dma((2, groups)),
            dma((2, groups)),
            dma((2, groups)),
            dma((groups, 4)),
            dma((groups, 4)),
            dma((groups,)),
            dma((groups,)),
        ],
        compiler_params=pltpu.CompilerParams(
            collective_id=0, has_side_effects=True, vmem_limit_bytes=48 * 1024 * 1024
        ),
    )(
        stretch_plan,
        segments.reshape(-1, rows),
        section_queries[0],
        section_keys[0],
        cascade_value_rows[0],
        output_grad[0],
    )
    place = lax.axis_index("pipe")
    section_output = jnp.where(place == 0, jnp.zeros_like(attended), attended)
    query_grad_sent = jnp.where(place == sizes[0] - 1, jnp.zeros_like(query_grad), query_grad)
    return section_output[None], query_grad_sent[None], key_grad[None], value_grad[None]


def solution(mesh):
    spread = P("pipe", ("ctx", "dp"), None)
    return jax.shard_map(
        functools.partial(_on_device, (mesh.shape["pipe"], mesh.shape["ctx"])),
        mesh=mesh,
        in_specs=(spread, spread, spread, spread, P(), P()),
        out_specs=(spread, spread, spread, spread),
        check_vma=False,
    )
```

```python
import functools
import math

import jax
import jax.numpy as jnp
from jax import lax
from jax.experimental import pallas as pl
from jax.experimental.pallas import tpu as pltpu
from jax.sharding import PartitionSpec as P

QUERY_HEADS = 32
KEY_VALUE_HEADS = 4
HEAD_SIZE = 128
GROUP = QUERY_HEADS // KEY_VALUE_HEADS
MESH = pl.DeviceIdType.MESH
F32 = jnp.float32
BF16 = jnp.bfloat16
LOW = -1e30


def _nt(a, b):
    return lax.dot_general(a, b, (((1,), (1,)), ((), ())), preferred_element_type=F32)


def _nn(a, b):
    return lax.dot_general(a, b, (((1,), (0,)), ((), ())), preferred_element_type=F32)


def _tn(a, b):
    return lax.dot_general(a, b, (((0,), (0,)), ((), ())), preferred_element_type=F32)


def one_of(index, choices):
    first, second, third, fourth = choices
    return lax.select(
        index < 2, lax.select(index == 0, first, second), lax.select(index == 2, third, fourth)
    )


def _kernel(
    sizes,
    plan_ref,
    seg_ref,
    q_hbm,
    k_hbm,
    v_hbm,
    do_hbm,
    so_out,
    qg_out,
    kg_out,
    vg_out,
    kv,
    qb,
    dob,
    att,
    dqb,
    bias,
    parts,
    loc,
    ret,
    back,
    psend,
    precv,
    loc_sem,
    kv_send,
    kv_recv,
    q_send,
    q_recv,
    out_send,
    out_recv,
    ret_send,
    ret_recv,
    fin_send,
    fin_recv,
    hello,
):
    n_pipe, n_ctx = sizes
    rows = k_hbm.shape[0]
    half = rows // 2
    width = GROUP * HEAD_SIZE
    window = 8 * half
    pad = 3 * half
    groups = KEY_VALUE_HEADS
    scale = 1.0 / math.sqrt(HEAD_SIZE)
    exp_scale = scale * math.log2(math.e)

    p = lax.axis_index("pipe")
    c = lax.axis_index("ctx")
    d = lax.axis_index("dp")
    me = 2 * c + d

    def at(dc, dd):
        return {"pipe": p, "ctx": lax.rem(c + dc + n_ctx, n_ctx), "dp": dd}

    other = at(0, 1 - d)
    across = at(2 * d - 1, 1 - d)
    up1, up2, down1, down2 = at(1, d), at(2, d), at(-1, d), at(-2, d)
    later = {"pipe": lax.rem(p + 1, n_pipe), "ctx": c, "dp": d}
    earlier = {"pipe": lax.rem(p + n_pipe - 1, n_pipe), "ctx": c, "dp": d}

    def remote(src, dst, send, recv, target):
        return pltpu.make_async_remote_copy(
            src_ref=src, dst_ref=dst, send_sem=send, recv_sem=recv, device_id=target, device_id_type=MESH
        )

    own = pl.ds(4 * rows, rows)
    kv_width = k_hbm.shape[1]
    own_k = pltpu.make_async_copy(k_hbm, kv.at[own, pl.ds(0, kv_width)], loc_sem.at[0])
    own_v = pltpu.make_async_copy(v_hbm, kv.at[own, pl.ds(kv_width, kv_width)], loc_sem.at[1])

    def own_q(g):
        return pltpu.make_async_copy(
            q_hbm.at[:, pl.ds(pl.multiple_of(g * width, width), width)],
            qb.at[g, pl.ds(half, rows)],
            loc_sem.at[2 + g],
        )

    def own_do(g):
        return pltpu.make_async_copy(
            do_hbm.at[:, pl.ds(pl.multiple_of(g * width, width), width)], dob.at[g], loc_sem.at[2 + groups + g]
        )

    own_k.start()
    own_v.start()
    for g in range(groups):
        own_q(g).start()
    for g in range(groups):
        own_do(g).start()

    barrier = pltpu.get_barrier_semaphore()
    not_first, not_last = p > 0, p < n_pipe - 1

    def signal(semaphore, target):
        pl.semaphore_signal(semaphore, inc=1, device_id=target, device_id_type=MESH)

    for target in (other, down1, down2):
        signal(barrier, target)

    @pl.when(d == 0)
    def _():
        signal(barrier, across)

    @pl.when(not_last)
    def _():
        signal(barrier, later)

    @pl.when(not_first)
    def _():
        signal(barrier, earlier)

    own_k.wait()
    own_v.wait()
    for g in range(groups):
        own_q(g).wait()
    pl.semaphore_wait(barrier, 3 + d + not_last.astype(jnp.int32) + not_first.astype(jnp.int32))
    signal(hello.at[0], up1)
    signal(hello.at[1], up2)

    @pl.when(d == 1)
    def _():
        signal(hello.at[2], across)


    def kv_copy(kind, source, place, target):
        return remote(
            kv.at[pl.ds(pl.multiple_of(source * rows, rows), rows)],
            kv.at[pl.ds(pl.multiple_of(place * rows, rows), rows)],
            kv_send.at[kind],
            kv_recv.at[kind],
            target,
        )

    kv_other = kv_copy(0, 4, 3 + 2 * d, other)
    kv_up1 = kv_copy(1, 4, 2, up1)
    kv_up2 = kv_copy(2, 4, 0, up2)
    kv_pass1 = kv_copy(3, 5 - 2 * d, 3 - 2 * d, up1)
    kv_pass2 = kv_copy(4, 5 - 2 * d, 1 + 4 * d, at(2 - 3 * d, d))

    def q_other(g):
        first, place = half * (2 - d), 3 * half * d
        return remote(
            qb.at[g, pl.ds(pl.multiple_of(first, half), half)],
            qb.at[g, pl.ds(pl.multiple_of(place, half), half)],
            q_send.at[0, g],
            q_recv.at[0, g],
            other,
        )

    def q_across(g):
        first, place = half * (1 + d), 3 * half * (1 - d)
        return remote(
            qb.at[g, pl.ds(pl.multiple_of(first, half), half)],
            qb.at[g, pl.ds(pl.multiple_of(place, half), half)],
            q_send.at[1, g],
            q_recv.at[1, g],
            across,
        )

    kv_other.start()
    kv_up1.start()
    kv_up2.start()
    q_other(0).start()
    q_other(1).start()

    zeros = jnp.zeros((pad, 2 * HEAD_SIZE), F32)
    shifts = []
    row_at = lax.broadcasted_iota(jnp.int32, seg_ref.shape, 0)
    for s in range(2):
        block = plan_ref[2 * me + s]
        shifts.append(block - 2 * me + 1)
        pair = lax.div(block, 2)
        line = jnp.sum(jnp.where(row_at == pair, seg_ref[...].astype(F32), 0.0), axis=0, keepdims=True)
        lane = lax.broadcasted_iota(jnp.int32, (half, rows), 1)
        sub = lax.broadcasted_iota(jnp.int32, (half, rows), 0)
        picked = jnp.where(lane == sub + (block - 2 * pair) * half, jnp.broadcast_to(line, (half, rows)), 0.0)
        mine = jnp.sum(picked, axis=1, keepdims=True)

        def count(r, total, mine=mine):
            row = seg_ref[pl.ds(r, 1), :].astype(F32)
            return total + jnp.where(row < mine, 1.0, 0.0)

        total = lax.fori_loop(0, seg_ref.shape[0], count, jnp.zeros((half, rows), F32))
        first = jnp.sum(total, axis=1, keepdims=True)
        key_at = lax.broadcasted_iota(jnp.int32, (half, window), 1) + (block - 7) * half
        query_at = lax.broadcasted_iota(jnp.int32, (half, window), 0) + block * half
        seen = (key_at.astype(F32) >= first) & (key_at <= query_at)
        bias[s] = jnp.where(seen, 0.0, LOW)
        parts[s, pl.ds(0, pad)] = zeros
        parts[s, pl.ds(pad + window, pad + rows - half)] = jnp.zeros((pad + rows - half, 2 * HEAD_SIZE), F32)

    @pl.when(d == 0)
    def _():
        pl.semaphore_wait(hello.at[2], 1)

    q_across(0).start()
    q_across(1).start()
    for g in range(2, groups):
        q_other(g).start()
        q_across(g).start()
    pl.semaphore_wait(hello.at[0], 1)
    pl.semaphore_wait(hello.at[1], 1)

    kv_other.wait_recv()
    kv_pass1.start()
    kv_pass2.start()
    for copy in (kv_up1, kv_up2, kv_pass1, kv_pass2):
        copy.wait_recv()
    for g in range(groups):
        own_do(g).wait()

    def columns(g):
        return pl.ds(pl.multiple_of(g * width, width), width)

    def att_copy(g):
        return remote(att.at[g], so_out.at[:, columns(g)], out_send.at[0, g], out_recv.at[0, g], later)

    def dq_copy(g):
        return remote(dqb.at[g], qg_out.at[:, columns(g)], out_send.at[1, g], out_recv.at[1, g], earlier)

    def ret_copy(g, kind):
        source, target = ((0, down2), (2, down1), (3 - 2 * d, down1), (1 + 4 * d, at(3 * d - 2, d)))[kind]
        return remote(ret.at[g, source], back.at[g, kind], ret_send.at[g, kind], ret_recv.at[g, kind], target)

    def fin_copy(g):
        return remote(psend.at[g], precv.at[g], fin_send.at[g], fin_recv.at[g], other)

    def window_part(o):
        total = None
        for s in range(2):
            starts = [pl.multiple_of(pad - k * half + o * rows, half) for k in range(4)]
            one = one_of(shifts[s], [parts[s, pl.ds(start, rows), :] for start in starts])
            total = one if total is None else total + one
        return total

    def pass_on(g):
        for kind in range(4):
            ret_copy(g, kind).wait_recv()
        total = loc[g, 1] + back[g, 2].astype(F32) + back[g, 3].astype(F32)
        psend[g] = total.astype(BF16)
        fin_copy(g).start()

    def one_group(g, carry):
        q_other(g).wait_recv()
        q_across(g).wait_recv()
        for s in range(2):
            shift = shifts[s]
            chosen = one_of(shift, [qb[g, pl.ds(k * half, half), :] for k in range(4)])
            grad = dob[g, pl.ds(s * half, half), :]
            heads = [slice(h * HEAD_SIZE, (h + 1) * HEAD_SIZE) for h in range(GROUP)]
            qs = jnp.concatenate([chosen[:, h] for h in heads], axis=0)
            gs = jnp.concatenate([grad[:, h] for h in heads], axis=0)
            k_place = pl.ds(pl.multiple_of(g * HEAD_SIZE, HEAD_SIZE), HEAD_SIZE)
            v_place = pl.ds(pl.multiple_of(kv_width + g * HEAD_SIZE, HEAD_SIZE), HEAD_SIZE)
            ks = one_of(shift, [kv[pl.ds(k * half, window), k_place] for k in range(4)])
            vs = one_of(shift, [kv[pl.ds(k * half, window), v_place] for k in range(4)])
            scores = _nt(qs, ks).reshape(GROUP, half, window) + bias[s][None]
            scores = scores.reshape(GROUP * half, window)
            top = jnp.max(scores, axis=1, keepdims=True)
            weights = jnp.exp2((scores - top) * exp_scale)
            probs = weights * (1.0 / jnp.sum(weights, axis=1, keepdims=True))
            low = probs.astype(BF16)
            attended = _nn(low, vs).astype(BF16)
            grad_probs = _nt(gs, vs)
            delta = jnp.sum(gs.astype(F32) * attended.astype(F32), axis=1, keepdims=True)
            grad_scores = (probs * (grad_probs - delta)).astype(BF16)
            query_grad = (_nn(grad_scores, ks) * scale).astype(BF16)
            for h in range(GROUP):
                att[g, pl.ds(s * half, half), heads[h]] = attended[h * half : (h + 1) * half]
                dqb[g, pl.ds(s * half, half), heads[h]] = query_grad[h * half : (h + 1) * half]
            parts[s, pl.ds(pad, window), pl.ds(0, HEAD_SIZE)] = _tn(grad_scores, qs) * scale
            parts[s, pl.ds(pad, window), pl.ds(HEAD_SIZE, HEAD_SIZE)] = _tn(low, gs)
        for o in range(6):
            ret[g, o] = window_part(o).astype(BF16)
        loc[g, 0] = window_part(4)
        loc[g, 1] = window_part(5 - 2 * d)
        for kind in range(4):
            ret_copy(g, kind).start()

        @pl.when(not_last)
        def _():
            att_copy(g).start()

        @pl.when(not_first)
        def _():
            dq_copy(g).start()

        @pl.when(g > 0)
        def _():
            pass_on(g - 1)

        return carry

    lax.fori_loop(0, groups, one_group, 0)
    pass_on(groups - 1)

    def finish(g, carry):
        fin_copy(g).wait_recv()
        total = loc[g, 0] + back[g, 0].astype(F32) + back[g, 1].astype(F32) + precv[g].astype(F32)
        place = pl.ds(pl.multiple_of(g * HEAD_SIZE, HEAD_SIZE), HEAD_SIZE)
        kg_out[:, place] = total[:, :HEAD_SIZE].astype(BF16)
        vg_out[:, place] = total[:, HEAD_SIZE:].astype(BF16)
        return carry

    lax.fori_loop(0, groups, finish, 0)

    for copy in (kv_other, kv_up1, kv_up2, kv_pass1, kv_pass2):
        copy.wait_send()

    def drain(g, carry):
        q_other(g).wait_send()
        q_across(g).wait_send()
        for kind in range(4):
            ret_copy(g, kind).wait_send()
        fin_copy(g).wait_send()

        @pl.when(not_last)
        def _():
            att_copy(g).wait_send()
            dq_copy(g).wait_recv()

        @pl.when(not_first)
        def _():
            dq_copy(g).wait_send()
            att_copy(g).wait_recv()

        return carry

    lax.fori_loop(0, groups, drain, 0)


def _on_device(sizes, section_queries, section_keys, cascade_value_rows, output_grad, segments, stretch_plan):
    _, rows, width = section_queries.shape
    kv_width = section_keys.shape[2]
    groups, half = KEY_VALUE_HEADS, rows // 2
    share = width // groups
    hbm = pl.BlockSpec(memory_space=pltpu.HBM)
    vmem = pl.BlockSpec(memory_space=pltpu.VMEM)
    dma = pltpu.SemaphoreType.DMA
    attended, query_grad, key_grad, value_grad = pl.pallas_call(
        functools.partial(_kernel, sizes),
        out_shape=[
            jax.ShapeDtypeStruct((rows, width), BF16),
            jax.ShapeDtypeStruct((rows, width), BF16),
            jax.ShapeDtypeStruct((rows, kv_width), BF16),
            jax.ShapeDtypeStruct((rows, kv_width), BF16),
        ],
        in_specs=[pl.BlockSpec(memory_space=pltpu.SMEM), vmem, hbm, hbm, hbm, hbm],
        out_specs=[hbm, hbm, vmem, vmem],
        scratch_shapes=[
            pltpu.VMEM((6 * rows, 2 * kv_width), BF16),
            pltpu.VMEM((groups, 2 * rows, share), BF16),
            pltpu.VMEM((groups, rows, share), BF16),
            pltpu.VMEM((groups, rows, share), BF16),
            pltpu.VMEM((groups, rows, share), BF16),
            pltpu.VMEM((2, half, 8 * half), F32),
            pltpu.VMEM((2, 14 * half + rows // 2, 2 * HEAD_SIZE), F32),
            pltpu.VMEM((groups, 2, rows, 2 * HEAD_SIZE), F32),
            pltpu.VMEM((groups, 6, rows, 2 * HEAD_SIZE), BF16),
            pltpu.VMEM((groups, 4, rows, 2 * HEAD_SIZE), BF16),
            pltpu.VMEM((groups, rows, 2 * HEAD_SIZE), BF16),
            pltpu.VMEM((groups, rows, 2 * HEAD_SIZE), BF16),
            dma((2 + 2 * groups,)),
            dma((5,)),
            dma((5,)),
            dma((2, groups)),
            dma((2, groups)),
            dma((2, groups)),
            dma((2, groups)),
            dma((groups, 4)),
            dma((groups, 4)),
            dma((groups,)),
            dma((groups,)),
            pltpu.SemaphoreType.REGULAR((3,)),
        ],
        compiler_params=pltpu.CompilerParams(
            collective_id=0, has_side_effects=True, vmem_limit_bytes=56 * 1024 * 1024
        ),
    )(
        stretch_plan,
        segments.reshape(-1, rows),
        section_queries[0],
        section_keys[0],
        cascade_value_rows[0],
        output_grad[0],
    )
    place = lax.axis_index("pipe")
    section_output = jnp.where(place == 0, jnp.zeros_like(attended), attended)
    query_grad_sent = jnp.where(place == sizes[0] - 1, jnp.zeros_like(query_grad), query_grad)
    return section_output[None], query_grad_sent[None], key_grad[None], value_grad[None]


def solution(mesh):
    spread = P("pipe", ("ctx", "dp"), None)
    return jax.shard_map(
        functools.partial(_on_device, (mesh.shape["pipe"], mesh.shape["ctx"])),
        mesh=mesh,
        in_specs=(spread, spread, spread, spread, P(), P()),
        out_specs=(spread, spread, spread, spread),
        check_vma=False,
    )
```

```python
import functools
import math

import jax
import jax.numpy as jnp
from jax import lax
from jax.experimental import pallas as pl
from jax.experimental.pallas import tpu as pltpu
from jax.sharding import PartitionSpec as P

QUERY_HEADS = 32
KEY_VALUE_HEADS = 4
HEAD_SIZE = 128
GROUP = QUERY_HEADS // KEY_VALUE_HEADS
MESH = pl.DeviceIdType.MESH
F32 = jnp.float32
BF16 = jnp.bfloat16
LOW = -1e30
PIECES = 4


def _nt(a, b):
    return lax.dot_general(a, b, (((1,), (1,)), ((), ())), preferred_element_type=F32)


def _nn(a, b):
    return lax.dot_general(a, b, (((1,), (0,)), ((), ())), preferred_element_type=F32)


def _tn(a, b):
    return lax.dot_general(a, b, (((0,), (0,)), ((), ())), preferred_element_type=F32)


def one_of(index, choices):
    first, second, third, fourth = choices
    return lax.select(
        index < 2, lax.select(index == 0, first, second), lax.select(index == 2, third, fourth)
    )


def _kernel(
    sizes,
    plan_ref,
    seg_ref,
    q_hbm,
    k_hbm,
    v_hbm,
    do_hbm,
    so_out,
    qg_out,
    kg_out,
    vg_out,
    kv,
    qb,
    dob,
    att,
    dqb,
    bias,
    parts,
    loc,
    ret,
    back,
    psend,
    precv,
    loc_sem,
    kv_send,
    kv_recv,
    q_send,
    q_recv,
    out_send,
    out_recv,
    ret_send,
    ret_recv,
    fin_send,
    fin_recv,
    hello,
):
    n_pipe, n_ctx = sizes
    rows = k_hbm.shape[0]
    half = rows // 2
    width = GROUP * HEAD_SIZE
    window = 8 * half
    pad = 3 * half
    groups = KEY_VALUE_HEADS
    scale = 1.0 / math.sqrt(HEAD_SIZE)
    exp_scale = scale * math.log2(math.e)

    p = lax.axis_index("pipe")
    c = lax.axis_index("ctx")
    d = lax.axis_index("dp")
    me = 2 * c + d

    def at(dc, dd):
        return {"pipe": p, "ctx": lax.rem(c + dc + n_ctx, n_ctx), "dp": dd}

    other = at(0, 1 - d)
    across = at(2 * d - 1, 1 - d)
    up1, up2, down1, down2 = at(1, d), at(2, d), at(-1, d), at(-2, d)
    later = {"pipe": lax.rem(p + 1, n_pipe), "ctx": c, "dp": d}
    earlier = {"pipe": lax.rem(p + n_pipe - 1, n_pipe), "ctx": c, "dp": d}

    def remote(src, dst, send, recv, target):
        return pltpu.make_async_remote_copy(
            src_ref=src, dst_ref=dst, send_sem=send, recv_sem=recv, device_id=target, device_id_type=MESH
        )

    own = pl.ds(4 * rows, rows)

    def own_kv(g):
        part = pl.ds(pl.multiple_of(g * HEAD_SIZE, HEAD_SIZE), HEAD_SIZE)
        return (
            pltpu.make_async_copy(k_hbm.at[:, part], kv.at[g, own, pl.ds(0, HEAD_SIZE)], loc_sem.at[0, g]),
            pltpu.make_async_copy(v_hbm.at[:, part], kv.at[g, own, pl.ds(HEAD_SIZE, HEAD_SIZE)], loc_sem.at[1, g]),
        )

    def own_q(g):
        return pltpu.make_async_copy(
            q_hbm.at[:, pl.ds(pl.multiple_of(g * width, width), width)],
            qb.at[g, pl.ds(half, rows)],
            loc_sem.at[2, g],
        )

    def own_do(g):
        return pltpu.make_async_copy(
            do_hbm.at[:, pl.ds(pl.multiple_of(g * width, width), width)], dob.at[g], loc_sem.at[3, g]
        )

    for g in range(groups):
        for copy in own_kv(g):
            copy.start()
    for g in range(groups):
        own_q(g).start()
    for g in range(groups):
        own_do(g).start()

    barrier = pltpu.get_barrier_semaphore()
    not_first, not_last = p > 0, p < n_pipe - 1

    def signal(semaphore, target):
        pl.semaphore_signal(semaphore, inc=1, device_id=target, device_id_type=MESH)

    for target in (other, down1, down2):
        signal(barrier, target)

    @pl.when(d == 0)
    def _():
        signal(barrier, across)

    @pl.when(not_last)
    def _():
        signal(barrier, later)

    @pl.when(not_first)
    def _():
        signal(barrier, earlier)

    for g in range(groups):
        for copy in own_kv(g):
            copy.wait()
        own_q(g).wait()
    pl.semaphore_wait(barrier, 3 + d + not_last.astype(jnp.int32) + not_first.astype(jnp.int32))
    signal(hello.at[0], up1)
    signal(hello.at[1], up2)

    @pl.when(d == 1)
    def _():
        signal(hello.at[2], across)


    def kv_copy(kind, g):
        source, place, target = (
            (4, 3 + 2 * d, other),
            (4, 2, up1),
            (4, 0, up2),
            (5 - 2 * d, 3 - 2 * d, up1),
            (5 - 2 * d, 1 + 4 * d, at(2 - 3 * d, d)),
        )[kind]
        return remote(
            kv.at[g, pl.ds(pl.multiple_of(source * rows, rows), rows)],
            kv.at[g, pl.ds(pl.multiple_of(place * rows, rows), rows)],
            kv_send.at[kind, g],
            kv_recv.at[kind, g],
            target,
        )

    def q_other(g):
        first, place = half * (2 - d), 3 * half * d
        return remote(
            qb.at[g, pl.ds(pl.multiple_of(first, half), half)],
            qb.at[g, pl.ds(pl.multiple_of(place, half), half)],
            q_send.at[0, g],
            q_recv.at[0, g],
            other,
        )

    def q_across(g):
        first, place = half * (1 + d), 3 * half * (1 - d)
        return remote(
            qb.at[g, pl.ds(pl.multiple_of(first, half), half)],
            qb.at[g, pl.ds(pl.multiple_of(place, half), half)],
            q_send.at[1, g],
            q_recv.at[1, g],
            across,
        )

    for g in range(groups):
        kv_copy(0, g).start()
    kv_copy(1, 0).start()
    kv_copy(2, 0).start()

    q_other(0).start()

    zeros = jnp.zeros((pad, 2 * HEAD_SIZE), F32)
    shifts = []
    row_at = lax.broadcasted_iota(jnp.int32, seg_ref.shape, 0)
    for s in range(2):
        block = plan_ref[2 * me + s]
        shifts.append(block - 2 * me + 1)
        pair = lax.div(block, 2)
        line = jnp.sum(jnp.where(row_at == pair, seg_ref[...].astype(F32), 0.0), axis=0, keepdims=True)
        lane = lax.broadcasted_iota(jnp.int32, (half, rows), 1)
        sub = lax.broadcasted_iota(jnp.int32, (half, rows), 0)
        picked = jnp.where(lane == sub + (block - 2 * pair) * half, jnp.broadcast_to(line, (half, rows)), 0.0)
        mine = jnp.sum(picked, axis=1, keepdims=True)

        def count(r, total, mine=mine):
            row = seg_ref[pl.ds(r, 1), :].astype(F32)
            return total + jnp.where(row < mine, 1.0, 0.0)

        total = lax.fori_loop(0, seg_ref.shape[0], count, jnp.zeros((half, rows), F32))
        first = jnp.sum(total, axis=1, keepdims=True)
        key_at = lax.broadcasted_iota(jnp.int32, (half, window), 1) + (block - 7) * half
        query_at = lax.broadcasted_iota(jnp.int32, (half, window), 0) + block * half
        seen = (key_at.astype(F32) >= first) & (key_at <= query_at)
        bias[s] = jnp.where(seen, 0.0, LOW)
        parts[s, pl.ds(0, pad)] = zeros
        parts[s, pl.ds(pad + window, pad + rows - half)] = jnp.zeros((pad + rows - half, 2 * HEAD_SIZE), F32)

    @pl.when(d == 0)
    def _():
        pl.semaphore_wait(hello.at[2], 1)

    q_across(0).start()
    for g in range(1, groups):
        q_other(g).start()
        q_across(g).start()
    pl.semaphore_wait(hello.at[0], 1)
    pl.semaphore_wait(hello.at[1], 1)

    def relay(g, carry):
        kv_copy(0, g).wait_recv()
        kv_copy(3, g).start()
        kv_copy(4, g).start()

        @pl.when(g + 1 < groups)
        def _():
            kv_copy(1, g + 1).start()
            kv_copy(2, g + 1).start()

        return carry

    lax.fori_loop(0, groups, relay, 0)
    for g in range(groups):
        own_do(g).wait()

    def columns(g):
        return pl.ds(pl.multiple_of(g * width, width), width)

    def att_copy(g):
        return remote(att.at[g], so_out.at[:, columns(g)], out_send.at[0, g], out_recv.at[0, g], later)

    def dq_copy(g):
        return remote(dqb.at[g], qg_out.at[:, columns(g)], out_send.at[1, g], out_recv.at[1, g], earlier)

    def ret_copy(g, kind):
        source, target = ((0, down2), (2, down1), (3 - 2 * d, down1), (1 + 4 * d, at(3 * d - 2, d)))[kind]
        return remote(ret.at[g, source], back.at[g, kind], ret_send.at[g, kind], ret_recv.at[g, kind], target)

    def fin_copy(g):
        return remote(psend.at[g], precv.at[g], fin_send.at[g], fin_recv.at[g], other)

    def window_part(o):
        total = None
        for s in range(2):
            starts = [pl.multiple_of(pad - k * half + o * rows, half) for k in range(4)]
            one = one_of(shifts[s], [parts[s, pl.ds(start, rows), :] for start in starts])
            total = one if total is None else total + one
        return total

    def pass_on(g):
        for kind in range(4):
            ret_copy(g, kind).wait_recv()
        total = loc[g, 1] + back[g, 2].astype(F32) + back[g, 3].astype(F32)
        psend[g] = total.astype(BF16)
        fin_copy(g).start()

    def one_group(g, carry):
        for kind in range(1, 5):
            kv_copy(kind, g).wait_recv()
        q_other(g).wait_recv()
        q_across(g).wait_recv()
        for s in range(2):
            shift = shifts[s]
            chosen = one_of(shift, [qb[g, pl.ds(k * half, half), :] for k in range(4)])
            grad = dob[g, pl.ds(s * half, half), :]
            heads = [slice(h * HEAD_SIZE, (h + 1) * HEAD_SIZE) for h in range(GROUP)]
            qs = jnp.concatenate([chosen[:, h] for h in heads], axis=0)
            gs = jnp.concatenate([grad[:, h] for h in heads], axis=0)
            ks = one_of(shift, [kv[g, pl.ds(k * half, window), pl.ds(0, HEAD_SIZE)] for k in range(4)])
            vs = one_of(shift, [kv[g, pl.ds(k * half, window), pl.ds(HEAD_SIZE, HEAD_SIZE)] for k in range(4)])
            scores = _nt(qs, ks).reshape(GROUP, half, window) + bias[s][None]
            scores = scores.reshape(GROUP * half, window)
            top = jnp.max(scores, axis=1, keepdims=True)
            weights = jnp.exp2((scores - top) * exp_scale)
            probs = weights * (1.0 / jnp.sum(weights, axis=1, keepdims=True))
            low = probs.astype(BF16)
            attended = _nn(low, vs).astype(BF16)
            grad_probs = _nt(gs, vs)
            delta = jnp.sum(gs.astype(F32) * attended.astype(F32), axis=1, keepdims=True)
            grad_scores = (probs * (grad_probs - delta)).astype(BF16)
            query_grad = (_nn(grad_scores, ks) * scale).astype(BF16)
            for h in range(GROUP):
                att[g, pl.ds(s * half, half), heads[h]] = attended[h * half : (h + 1) * half]
                dqb[g, pl.ds(s * half, half), heads[h]] = query_grad[h * half : (h + 1) * half]
            parts[s, pl.ds(pad, window), pl.ds(0, HEAD_SIZE)] = _tn(grad_scores, qs) * scale
            parts[s, pl.ds(pad, window), pl.ds(HEAD_SIZE, HEAD_SIZE)] = _tn(low, gs)
        for o in range(6):
            ret[g, o] = window_part(o).astype(BF16)
        loc[g, 0] = window_part(4)
        loc[g, 1] = window_part(5 - 2 * d)
        for kind in range(4):
            ret_copy(g, kind).start()

        @pl.when(not_last)
        def _():
            att_copy(g).start()

        @pl.when(not_first)
        def _():
            dq_copy(g).start()

        @pl.when(g > 0)
        def _():
            pass_on(g - 1)

        return carry

    lax.fori_loop(0, groups, one_group, 0)
    pass_on(groups - 1)

    def finish(g, carry):
        fin_copy(g).wait_recv()
        total = loc[g, 0] + back[g, 0].astype(F32) + back[g, 1].astype(F32) + precv[g].astype(F32)
        place = pl.ds(pl.multiple_of(g * HEAD_SIZE, HEAD_SIZE), HEAD_SIZE)
        kg_out[:, place] = total[:, :HEAD_SIZE].astype(BF16)
        vg_out[:, place] = total[:, HEAD_SIZE:].astype(BF16)
        return carry

    lax.fori_loop(0, groups, finish, 0)

    def drain(g, carry):
        for kind in range(5):
            kv_copy(kind, g).wait_send()
        q_other(g).wait_send()
        q_across(g).wait_send()
        for kind in range(4):
            ret_copy(g, kind).wait_send()
        fin_copy(g).wait_send()

        @pl.when(not_last)
        def _():
            att_copy(g).wait_send()
            dq_copy(g).wait_recv()

        @pl.when(not_first)
        def _():
            dq_copy(g).wait_send()
            att_copy(g).wait_recv()

        return carry

    lax.fori_loop(0, groups, drain, 0)


def _place(sizes, so_in, qg_in, kg_in, vg_in, so_out, qg_out, kg_out, vg_out, so, qg, kg, vg, in_sem, out_sem):
    p = lax.axis_index("pipe")
    moves = []
    for source, buffer, to, none in (
        (so_in, so, so_out, 0),
        (qg_in, qg, qg_out, sizes[0] - 1),
        (kg_in, kg, kg_out, None),
        (vg_in, vg, vg_out, None),
    ):
        pieces = 1 if none is None else PIECES
        step = source.shape[0] // pieces
        for k in range(pieces):
            part, n = pl.ds(k * step, step), len(moves)
            moves.append(
                (
                    pltpu.make_async_copy(source.at[part], buffer.at[part], in_sem.at[n]),
                    pltpu.make_async_copy(buffer.at[part], to.at[part], out_sem.at[n]),
                    none,
                    buffer.at[part],
                )
            )
    for load, _, _, _ in moves:
        load.start()
    for load, store, none, buffer in moves:
        load.wait()
        if none is not None:

            @pl.when(p == none)
            def _(buffer=buffer):
                buffer[...] = jnp.zeros(buffer.shape, buffer.dtype)

        store.start()
    for _, store, _, _ in moves:
        store.wait()


def _on_device(sizes, section_queries, section_keys, cascade_value_rows, output_grad, segments, stretch_plan):
    _, rows, width = section_queries.shape
    kv_width = section_keys.shape[2]
    groups, half = KEY_VALUE_HEADS, rows // 2
    share = width // groups
    hbm = pl.BlockSpec(memory_space=pltpu.HBM)
    vmem = pl.BlockSpec(memory_space=pltpu.VMEM)
    dma = pltpu.SemaphoreType.DMA
    attended, query_grad, key_grad, value_grad = pl.pallas_call(
        functools.partial(_kernel, sizes),
        out_shape=[
            jax.ShapeDtypeStruct((rows, width), BF16),
            jax.ShapeDtypeStruct((rows, width), BF16),
            jax.ShapeDtypeStruct((rows, kv_width), BF16),
            jax.ShapeDtypeStruct((rows, kv_width), BF16),
        ],
        in_specs=[pl.BlockSpec(memory_space=pltpu.SMEM), vmem, hbm, hbm, hbm, hbm],
        out_specs=[hbm, hbm, vmem, vmem],
        scratch_shapes=[
            pltpu.VMEM((groups, 6 * rows, 2 * HEAD_SIZE), BF16),
            pltpu.VMEM((groups, 2 * rows, share), BF16),
            pltpu.VMEM((groups, rows, share), BF16),
            pltpu.VMEM((groups, rows, share), BF16),
            pltpu.VMEM((groups, rows, share), BF16),
            pltpu.VMEM((2, half, 8 * half), F32),
            pltpu.VMEM((2, 14 * half + rows // 2, 2 * HEAD_SIZE), F32),
            pltpu.VMEM((groups, 2, rows, 2 * HEAD_SIZE), F32),
            pltpu.VMEM((groups, 6, rows, 2 * HEAD_SIZE), BF16),
            pltpu.VMEM((groups, 4, rows, 2 * HEAD_SIZE), BF16),
            pltpu.VMEM((groups, rows, 2 * HEAD_SIZE), BF16),
            pltpu.VMEM((groups, rows, 2 * HEAD_SIZE), BF16),
            dma((4, groups)),
            dma((5, groups)),
            dma((5, groups)),
            dma((2, groups)),
            dma((2, groups)),
            dma((2, groups)),
            dma((2, groups)),
            dma((groups, 4)),
            dma((groups, 4)),
            dma((groups,)),
            dma((groups,)),
            pltpu.SemaphoreType.REGULAR((3,)),
        ],
        compiler_params=pltpu.CompilerParams(
            collective_id=0, has_side_effects=True, vmem_limit_bytes=56 * 1024 * 1024
        ),
    )(
        stretch_plan,
        segments.reshape(-1, rows),
        section_queries[0],
        section_keys[0],
        cascade_value_rows[0],
        output_grad[0],
    )
    section_output, query_grad_sent, key_grad, value_grad = pl.pallas_call(
        functools.partial(_place, sizes),
        out_shape=[
            jax.ShapeDtypeStruct((rows, width), BF16),
            jax.ShapeDtypeStruct((rows, width), BF16),
            jax.ShapeDtypeStruct((rows, kv_width), BF16),
            jax.ShapeDtypeStruct((rows, kv_width), BF16),
        ],
        in_specs=[hbm] * 4,
        out_specs=[hbm] * 4,
        scratch_shapes=[
            pltpu.VMEM((rows, width), BF16),
            pltpu.VMEM((rows, width), BF16),
            pltpu.VMEM((rows, kv_width), BF16),
            pltpu.VMEM((rows, kv_width), BF16),
            dma((2 * PIECES + 2,)),
            dma((2 * PIECES + 2,)),
        ],
        compiler_params=pltpu.CompilerParams(vmem_limit_bytes=56 * 1024 * 1024),
    )(attended, query_grad, key_grad, value_grad)
    return section_output[None], query_grad_sent[None], key_grad[None], value_grad[None]


def solution(mesh):
    spread = P("pipe", ("ctx", "dp"), None)
    return jax.shard_map(
        functools.partial(_on_device, (mesh.shape["pipe"], mesh.shape["ctx"])),
        mesh=mesh,
        in_specs=(spread, spread, spread, spread, P(), P()),
        out_specs=(spread, spread, spread, spread),
        check_vma=False,
    )
```

```python
import functools
import math

import jax
import jax.numpy as jnp
from jax import lax
from jax.experimental import pallas as pl
from jax.experimental.pallas import tpu as pltpu
from jax.sharding import PartitionSpec as P

QUERY_HEADS = 32
KEY_VALUE_HEADS = 4
HEAD_SIZE = 128
GROUP = QUERY_HEADS // KEY_VALUE_HEADS
MESH = pl.DeviceIdType.MESH
F32 = jnp.float32
BF16 = jnp.bfloat16
LOW = -1e30
PIECES = 4


def _nt(a, b):
    return lax.dot_general(a, b, (((1,), (1,)), ((), ())), preferred_element_type=F32)


def _nn(a, b):
    return lax.dot_general(a, b, (((1,), (0,)), ((), ())), preferred_element_type=F32)


def _tn(a, b):
    return lax.dot_general(a, b, (((0,), (0,)), ((), ())), preferred_element_type=F32)


def one_of(index, choices):
    first, second, third, fourth = choices
    return lax.select(
        index < 2, lax.select(index == 0, first, second), lax.select(index == 2, third, fourth)
    )


def _kernel(
    sizes,
    plan_hbm,
    seg_hbm,
    q_hbm,
    k_hbm,
    v_hbm,
    do_hbm,
    so_out,
    qg_out,
    kg_out,
    vg_out,
    plan_ref,
    seg_ref,
    kv,
    qb,
    dob,
    att,
    dqb,
    bias,
    parts,
    loc,
    ret,
    back,
    psend,
    precv,
    loc_sem,
    kv_send,
    kv_recv,
    q_send,
    q_recv,
    out_send,
    out_recv,
    ret_send,
    ret_recv,
    fin_send,
    fin_recv,
    hello,
):
    n_pipe, n_ctx = sizes
    rows = k_hbm.shape[0]
    half = rows // 2
    width = GROUP * HEAD_SIZE
    window = 8 * half
    pad = 3 * half
    groups = KEY_VALUE_HEADS
    scale = 1.0 / math.sqrt(HEAD_SIZE)
    exp_scale = scale * math.log2(math.e)

    p = lax.axis_index("pipe")
    c = lax.axis_index("ctx")
    d = lax.axis_index("dp")
    me = 2 * c + d

    def at(dc, dd):
        return {"pipe": p, "ctx": lax.rem(c + dc + n_ctx, n_ctx), "dp": dd}

    other = at(0, 1 - d)
    across = at(2 * d - 1, 1 - d)
    up1, up2, down1, down2 = at(1, d), at(2, d), at(-1, d), at(-2, d)
    later = {"pipe": lax.rem(p + 1, n_pipe), "ctx": c, "dp": d}
    earlier = {"pipe": lax.rem(p + n_pipe - 1, n_pipe), "ctx": c, "dp": d}

    def remote(src, dst, send, recv, target):
        return pltpu.make_async_remote_copy(
            src_ref=src, dst_ref=dst, send_sem=send, recv_sem=recv, device_id=target, device_id_type=MESH
        )

    own = pl.ds(4 * rows, rows)

    def own_kv(g):
        part = pl.ds(pl.multiple_of(g * HEAD_SIZE, HEAD_SIZE), HEAD_SIZE)
        return (
            pltpu.make_async_copy(k_hbm.at[:, part], kv.at[g, own, pl.ds(0, HEAD_SIZE)], loc_sem.at[0, g]),
            pltpu.make_async_copy(v_hbm.at[:, part], kv.at[g, own, pl.ds(HEAD_SIZE, HEAD_SIZE)], loc_sem.at[1, g]),
        )

    def own_q(g):
        return pltpu.make_async_copy(
            q_hbm.at[:, pl.ds(pl.multiple_of(g * width, width), width)],
            qb.at[g, pl.ds(half, rows)],
            loc_sem.at[2, g],
        )

    def own_do(g):
        return pltpu.make_async_copy(
            do_hbm.at[:, pl.ds(pl.multiple_of(g * width, width), width)], dob.at[g], loc_sem.at[3, g]
        )

    barrier = pltpu.get_barrier_semaphore()
    not_first, not_last = p > 0, p < n_pipe - 1

    def signal(semaphore, target):
        pl.semaphore_signal(semaphore, inc=1, device_id=target, device_id_type=MESH)

    for target in (other, down1, down2):
        signal(barrier, target)

    @pl.when(d == 0)
    def _():
        signal(barrier, across)

    @pl.when(not_last)
    def _():
        signal(barrier, later)

    @pl.when(not_first)
    def _():
        signal(barrier, earlier)

    plan_copy = pltpu.make_async_copy(plan_hbm, plan_ref, loc_sem.at[4, 0])
    seg_copy = pltpu.make_async_copy(seg_hbm, seg_ref, loc_sem.at[4, 1])
    for g in range(groups):
        for copy in own_kv(g):
            copy.start()
    for g in range(groups):
        own_q(g).start()
    for g in range(groups):
        own_do(g).start()
    plan_copy.start()
    seg_copy.start()

    for g in range(groups):
        for copy in own_kv(g):
            copy.wait()
        own_q(g).wait()
    pl.semaphore_wait(barrier, 3 + d + not_last.astype(jnp.int32) + not_first.astype(jnp.int32))
    signal(hello.at[0], up1)
    signal(hello.at[1], up2)

    @pl.when(d == 1)
    def _():
        signal(hello.at[2], across)


    def kv_copy(kind, g):
        source, place, target = (
            (4, 3 + 2 * d, other),
            (4, 2, up1),
            (4, 0, up2),
            (5 - 2 * d, 3 - 2 * d, up1),
            (5 - 2 * d, 1 + 4 * d, at(2 - 3 * d, d)),
        )[kind]
        return remote(
            kv.at[g, pl.ds(pl.multiple_of(source * rows, rows), rows)],
            kv.at[g, pl.ds(pl.multiple_of(place * rows, rows), rows)],
            kv_send.at[kind, g],
            kv_recv.at[kind, g],
            target,
        )

    def q_other(g):
        first, place = half * (2 - d), 3 * half * d
        return remote(
            qb.at[g, pl.ds(pl.multiple_of(first, half), half)],
            qb.at[g, pl.ds(pl.multiple_of(place, half), half)],
            q_send.at[0, g],
            q_recv.at[0, g],
            other,
        )

    def q_across(g):
        first, place = half * (1 + d), 3 * half * (1 - d)
        return remote(
            qb.at[g, pl.ds(pl.multiple_of(first, half), half)],
            qb.at[g, pl.ds(pl.multiple_of(place, half), half)],
            q_send.at[1, g],
            q_recv.at[1, g],
            across,
        )

    for g in range(groups):
        kv_copy(0, g).start()
    kv_copy(1, 0).start()
    kv_copy(2, 0).start()

    q_other(0).start()

    plan_copy.wait()
    seg_copy.wait()
    zeros = jnp.zeros((pad, 2 * HEAD_SIZE), F32)
    shifts = []
    row_at = lax.broadcasted_iota(jnp.int32, seg_ref.shape, 0)
    for s in range(2):
        block = plan_ref[2 * me + s]
        shifts.append(block - 2 * me + 1)
        pair = lax.div(block, 2)
        line = jnp.sum(jnp.where(row_at == pair, seg_ref[...].astype(F32), 0.0), axis=0, keepdims=True)
        lane = lax.broadcasted_iota(jnp.int32, (half, rows), 1)
        sub = lax.broadcasted_iota(jnp.int32, (half, rows), 0)
        picked = jnp.where(lane == sub + (block - 2 * pair) * half, jnp.broadcast_to(line, (half, rows)), 0.0)
        mine = jnp.sum(picked, axis=1, keepdims=True)

        def count(r, total, mine=mine):
            row = seg_ref[pl.ds(r, 1), :].astype(F32)
            return total + jnp.where(row < mine, 1.0, 0.0)

        total = lax.fori_loop(0, seg_ref.shape[0], count, jnp.zeros((half, rows), F32))
        first = jnp.sum(total, axis=1, keepdims=True)
        key_at = lax.broadcasted_iota(jnp.int32, (half, window), 1) + (block - 7) * half
        query_at = lax.broadcasted_iota(jnp.int32, (half, window), 0) + block * half
        seen = (key_at.astype(F32) >= first) & (key_at <= query_at)
        bias[s] = jnp.where(seen, 0.0, LOW)
        parts[s, pl.ds(0, pad)] = zeros
        parts[s, pl.ds(pad + window, pad + rows - half)] = jnp.zeros((pad + rows - half, 2 * HEAD_SIZE), F32)

    @pl.when(d == 0)
    def _():
        pl.semaphore_wait(hello.at[2], 1)

    q_across(0).start()
    for g in range(1, groups):
        q_other(g).start()
        q_across(g).start()
    pl.semaphore_wait(hello.at[0], 1)
    pl.semaphore_wait(hello.at[1], 1)

    def relay(g, carry):
        kv_copy(0, g).wait_recv()
        kv_copy(3, g).start()
        kv_copy(4, g).start()

        @pl.when(g + 1 < groups)
        def _():
            kv_copy(1, g + 1).start()
            kv_copy(2, g + 1).start()

        return carry

    lax.fori_loop(0, groups, relay, 0)
    for g in range(groups):
        own_do(g).wait()

    def columns(g):
        return pl.ds(pl.multiple_of(g * width, width), width)

    def att_copy(g):
        return remote(att.at[g], so_out.at[:, columns(g)], out_send.at[0, g], out_recv.at[0, g], later)

    def dq_copy(g):
        return remote(dqb.at[g], qg_out.at[:, columns(g)], out_send.at[1, g], out_recv.at[1, g], earlier)

    def ret_copy(g, kind):
        source, target = ((0, down2), (2, down1), (3 - 2 * d, down1), (1 + 4 * d, at(3 * d - 2, d)))[kind]
        return remote(ret.at[g, source], back.at[g, kind], ret_send.at[g, kind], ret_recv.at[g, kind], target)

    def fin_copy(g):
        return remote(psend.at[g], precv.at[g], fin_send.at[g], fin_recv.at[g], other)

    def window_part(o):
        total = None
        for s in range(2):
            starts = [pl.multiple_of(pad - k * half + o * rows, half) for k in range(4)]
            one = one_of(shifts[s], [parts[s, pl.ds(start, rows), :] for start in starts])
            total = one if total is None else total + one
        return total

    def pass_on(g):
        for kind in range(4):
            ret_copy(g, kind).wait_recv()
        total = loc[g, 1] + back[g, 2].astype(F32) + back[g, 3].astype(F32)
        psend[g] = total.astype(BF16)
        fin_copy(g).start()

    behind = (lax.rem(p, 4) == 1) | (lax.rem(p, 4) == 2)

    def one_group(g, carry):
        for kind in range(1, 5):
            kv_copy(kind, g).wait_recv()
        q_other(g).wait_recv()
        q_across(g).wait_recv()
        for s in range(2):
            shift = shifts[s]
            chosen = one_of(shift, [qb[g, pl.ds(k * half, half), :] for k in range(4)])
            grad = dob[g, pl.ds(s * half, half), :]
            heads = [slice(h * HEAD_SIZE, (h + 1) * HEAD_SIZE) for h in range(GROUP)]
            qs = jnp.concatenate([chosen[:, h] for h in heads], axis=0)
            gs = jnp.concatenate([grad[:, h] for h in heads], axis=0)
            ks = one_of(shift, [kv[g, pl.ds(k * half, window), pl.ds(0, HEAD_SIZE)] for k in range(4)])
            vs = one_of(shift, [kv[g, pl.ds(k * half, window), pl.ds(HEAD_SIZE, HEAD_SIZE)] for k in range(4)])
            scores = _nt(qs, ks).reshape(GROUP, half, window) + bias[s][None]
            scores = scores.reshape(GROUP * half, window)
            top = jnp.max(scores, axis=1, keepdims=True)
            weights = jnp.exp2((scores - top) * exp_scale)
            probs = weights * (1.0 / jnp.sum(weights, axis=1, keepdims=True))
            low = probs.astype(BF16)
            attended = _nn(low, vs).astype(BF16)
            grad_probs = _nt(gs, vs)
            delta = jnp.sum(gs.astype(F32) * attended.astype(F32), axis=1, keepdims=True)
            grad_scores = (probs * (grad_probs - delta)).astype(BF16)
            query_grad = (_nn(grad_scores, ks) * scale).astype(BF16)
            for h in range(GROUP):
                att[g, pl.ds(s * half, half), heads[h]] = attended[h * half : (h + 1) * half]
                dqb[g, pl.ds(s * half, half), heads[h]] = query_grad[h * half : (h + 1) * half]
            parts[s, pl.ds(pad, window), pl.ds(0, HEAD_SIZE)] = _tn(grad_scores, qs) * scale
            parts[s, pl.ds(pad, window), pl.ds(HEAD_SIZE, HEAD_SIZE)] = _tn(low, gs)
        for o in range(6):
            ret[g, o] = window_part(o).astype(BF16)
        loc[g, 0] = window_part(4)
        loc[g, 1] = window_part(5 - 2 * d)
        for kind in range(4):
            ret_copy(g, kind).start()

        @pl.when(not_last & ((g < groups - 1) | jnp.logical_not(behind)))
        def _():
            att_copy(g).start()

        @pl.when(not_first & ((g < groups - 1) | jnp.logical_not(behind)))
        def _():
            dq_copy(g).start()

        @pl.when(g > 1)
        def _():
            pass_on(g - 2)

        return carry

    lax.fori_loop(0, groups, one_group, 0)
    pass_on(groups - 2)
    pass_on(groups - 1)

    @pl.when(not_last & behind)
    def _():
        att_copy(groups - 1).start()

    @pl.when(not_first & behind)
    def _():
        dq_copy(groups - 1).start()


    def finish(g, carry):
        fin_copy(g).wait_recv()
        total = loc[g, 0] + back[g, 0].astype(F32) + back[g, 1].astype(F32) + precv[g].astype(F32)
        place = pl.ds(pl.multiple_of(g * HEAD_SIZE, HEAD_SIZE), HEAD_SIZE)
        kg_out[:, place] = total[:, :HEAD_SIZE].astype(BF16)
        vg_out[:, place] = total[:, HEAD_SIZE:].astype(BF16)
        return carry

    lax.fori_loop(0, groups, finish, 0)

    def drain(g, carry):
        for kind in range(5):
            kv_copy(kind, g).wait_send()
        q_other(g).wait_send()
        q_across(g).wait_send()
        for kind in range(4):
            ret_copy(g, kind).wait_send()
        fin_copy(g).wait_send()

        @pl.when(not_last)
        def _():
            att_copy(g).wait_send()
            dq_copy(g).wait_recv()

        @pl.when(not_first)
        def _():
            dq_copy(g).wait_send()
            att_copy(g).wait_recv()

        return carry

    lax.fori_loop(0, groups, drain, 0)


def _place(sizes, so_in, qg_in, kg_in, vg_in, so_out, qg_out, kg_out, vg_out, empty, sem):
    p = lax.axis_index("pipe")
    step = so_in.shape[0] // PIECES

    def pieces(source, to, first):
        return [
            pltpu.make_async_copy(source.at[pl.ds(k * step, step)], to.at[pl.ds(k * step, step)], sem.at[first + k])
            for k in range(PIECES)
        ]

    small = [
        pltpu.make_async_copy(kg_in, kg_out, sem.at[2 * PIECES]),
        pltpu.make_async_copy(vg_in, vg_out, sem.at[2 * PIECES + 1]),
    ]
    for source, to, first, none in ((so_in, so_out, 0, 0), (qg_in, qg_out, PIECES, sizes[0] - 1)):

        @pl.when(p != none)
        def _(source=source, to=to, first=first):
            for copy in pieces(source, to, first):
                copy.start()

        @pl.when(p == none)
        def _(to=to, first=first):
            empty[...] = jnp.zeros_like(empty)
            for copy in pieces(empty, to, first):
                copy.start()

    for copy in small:
        copy.start()
    for copy in pieces(so_in, so_out, 0) + pieces(qg_in, qg_out, PIECES) + small:
        copy.wait()


def _on_device(sizes, section_queries, section_keys, cascade_value_rows, output_grad, segments, stretch_plan):
    _, rows, width = section_queries.shape
    kv_width = section_keys.shape[2]
    groups, half = KEY_VALUE_HEADS, rows // 2
    share = width // groups
    hbm = pl.BlockSpec(memory_space=pltpu.HBM)
    vmem = pl.BlockSpec(memory_space=pltpu.VMEM)
    dma = pltpu.SemaphoreType.DMA
    attended, query_grad, key_grad, value_grad = pl.pallas_call(
        functools.partial(_kernel, sizes),
        out_shape=[
            pltpu.VMEM((rows, width), BF16),
            pltpu.VMEM((rows, width), BF16),
            pltpu.VMEM((rows, kv_width), BF16),
            pltpu.VMEM((rows, kv_width), BF16),
        ],
        in_specs=[hbm] * 6,
        out_specs=[vmem] * 4,
        scratch_shapes=[
            pltpu.SMEM(stretch_plan.shape, jnp.int32),
            pltpu.VMEM((segments.shape[0] // rows, rows), jnp.int32),
            pltpu.VMEM((groups, 6 * rows, 2 * HEAD_SIZE), BF16),
            pltpu.VMEM((groups, 2 * rows, share), BF16),
            pltpu.VMEM((groups, rows, share), BF16),
            pltpu.VMEM((groups, rows, share), BF16),
            pltpu.VMEM((groups, rows, share), BF16),
            pltpu.VMEM((2, half, 8 * half), F32),
            pltpu.VMEM((2, 14 * half + rows // 2, 2 * HEAD_SIZE), F32),
            pltpu.VMEM((groups, 2, rows, 2 * HEAD_SIZE), F32),
            pltpu.VMEM((groups, 6, rows, 2 * HEAD_SIZE), BF16),
            pltpu.VMEM((groups, 4, rows, 2 * HEAD_SIZE), BF16),
            pltpu.VMEM((groups, rows, 2 * HEAD_SIZE), BF16),
            pltpu.VMEM((groups, rows, 2 * HEAD_SIZE), BF16),
            dma((5, groups)),
            dma((5, groups)),
            dma((5, groups)),
            dma((2, groups)),
            dma((2, groups)),
            dma((2, groups)),
            dma((2, groups)),
            dma((groups, 4)),
            dma((groups, 4)),
            dma((groups,)),
            dma((groups,)),
            pltpu.SemaphoreType.REGULAR((3,)),
        ],
        compiler_params=pltpu.CompilerParams(
            collective_id=0, has_side_effects=True, vmem_limit_bytes=40 * 1024 * 1024
        ),
    )(
        *(
            pltpu.with_memory_space_constraint(value, pltpu.HBM)
            for value in (
                stretch_plan,
                segments.reshape(-1, rows),
                section_queries[0],
                section_keys[0],
                cascade_value_rows[0],
                output_grad[0],
            )
        )
    )
    section_output, query_grad_sent, key_grad, value_grad = pl.pallas_call(
        functools.partial(_place, sizes),
        out_shape=[
            jax.ShapeDtypeStruct((rows, width), BF16),
            jax.ShapeDtypeStruct((rows, width), BF16),
            jax.ShapeDtypeStruct((rows, kv_width), BF16),
            jax.ShapeDtypeStruct((rows, kv_width), BF16),
        ],
        in_specs=[vmem] * 4,
        out_specs=[hbm] * 4,
        scratch_shapes=[pltpu.VMEM((rows, width), BF16), dma((2 * PIECES + 2,))],
        compiler_params=pltpu.CompilerParams(vmem_limit_bytes=16 * 1024 * 1024),
    )(attended, query_grad, key_grad, value_grad)
    return section_output[None], query_grad_sent[None], key_grad[None], value_grad[None]


def solution(mesh):
    spread = P("pipe", ("ctx", "dp"), None)
    return jax.shard_map(
        functools.partial(_on_device, (mesh.shape["pipe"], mesh.shape["ctx"])),
        mesh=mesh,
        in_specs=(spread, spread, spread, spread, P(), P()),
        out_specs=(spread, spread, spread, spread),
        check_vma=False,
    )
```

```python
import functools
import math

import jax
import jax.numpy as jnp
from jax import lax
from jax.experimental import pallas as pl
from jax.experimental.pallas import tpu as pltpu
from jax.sharding import PartitionSpec as P

QUERY_HEADS = 32
KEY_VALUE_HEADS = 4
HEAD_SIZE = 128
GROUP = QUERY_HEADS // KEY_VALUE_HEADS
MESH = pl.DeviceIdType.MESH
F32 = jnp.float32
BF16 = jnp.bfloat16
LOW = -1e30
PIECES = 4


def _nt(a, b):
    return lax.dot_general(a, b, (((1,), (1,)), ((), ())), preferred_element_type=F32)


def _nn(a, b):
    return lax.dot_general(a, b, (((1,), (0,)), ((), ())), preferred_element_type=F32)


def _tn(a, b):
    return lax.dot_general(a, b, (((0,), (0,)), ((), ())), preferred_element_type=F32)


def one_of(index, choices):
    first, second, third, fourth = choices
    return lax.select(
        index < 2, lax.select(index == 0, first, second), lax.select(index == 2, third, fourth)
    )


def _kernel(
    sizes,
    plan_hbm,
    seg_hbm,
    q_hbm,
    k_hbm,
    v_hbm,
    do_hbm,
    so_out,
    qg_out,
    kg_out,
    vg_out,
    plan_ref,
    seg_ref,
    kv,
    qb,
    dob,
    att,
    dqb,
    bias,
    parts,
    loc,
    ret,
    back,
    psend,
    precv,
    loc_sem,
    kv_send,
    kv_recv,
    q_send,
    q_recv,
    out_send,
    out_recv,
    ret_send,
    ret_recv,
    fin_send,
    fin_recv,
    hello,
):
    n_pipe, n_ctx = sizes
    rows = k_hbm.shape[0]
    half = rows // 2
    width = GROUP * HEAD_SIZE
    window = 8 * half
    pad = 3 * half
    groups = KEY_VALUE_HEADS
    scale = 1.0 / math.sqrt(HEAD_SIZE)
    exp_scale = scale * math.log2(math.e)

    p = lax.axis_index("pipe")
    c = lax.axis_index("ctx")
    d = lax.axis_index("dp")
    me = 2 * c + d

    def at(dc, dd):
        return {"pipe": p, "ctx": lax.rem(c + dc + n_ctx, n_ctx), "dp": dd}

    other = at(0, 1 - d)
    across = at(2 * d - 1, 1 - d)
    up1, up2, down1, down2 = at(1, d), at(2, d), at(-1, d), at(-2, d)
    later = {"pipe": lax.rem(p + 1, n_pipe), "ctx": c, "dp": d}
    earlier = {"pipe": lax.rem(p + n_pipe - 1, n_pipe), "ctx": c, "dp": d}

    def remote(src, dst, send, recv, target):
        return pltpu.make_async_remote_copy(
            src_ref=src, dst_ref=dst, send_sem=send, recv_sem=recv, device_id=target, device_id_type=MESH
        )

    own = pl.ds(4 * rows, rows)

    def own_kv(g):
        part = pl.ds(pl.multiple_of(g * HEAD_SIZE, HEAD_SIZE), HEAD_SIZE)
        return (
            pltpu.make_async_copy(k_hbm.at[:, part], kv.at[g, own, pl.ds(0, HEAD_SIZE)], loc_sem.at[0, g]),
            pltpu.make_async_copy(v_hbm.at[:, part], kv.at[g, own, pl.ds(HEAD_SIZE, HEAD_SIZE)], loc_sem.at[1, g]),
        )

    def own_q(g):
        return pltpu.make_async_copy(
            q_hbm.at[:, pl.ds(pl.multiple_of(g * width, width), width)],
            qb.at[g, pl.ds(half, rows)],
            loc_sem.at[2, g],
        )

    def own_do(g):
        return pltpu.make_async_copy(
            do_hbm.at[:, pl.ds(pl.multiple_of(g * width, width), width)], dob.at[g], loc_sem.at[3, g]
        )

    barrier = pltpu.get_barrier_semaphore()
    not_first, not_last = p > 0, p < n_pipe - 1

    def signal(semaphore, target):
        pl.semaphore_signal(semaphore, inc=1, device_id=target, device_id_type=MESH)

    for target in (other, down1, down2):
        signal(barrier, target)

    @pl.when(d == 0)
    def _():
        signal(barrier, across)

    @pl.when(not_last)
    def _():
        signal(barrier, later)

    @pl.when(not_first)
    def _():
        signal(barrier, earlier)

    plan_copy = pltpu.make_async_copy(plan_hbm, plan_ref, loc_sem.at[4, 0])
    seg_copy = pltpu.make_async_copy(seg_hbm, seg_ref, loc_sem.at[4, 1])
    for g in range(groups):
        for copy in own_kv(g):
            copy.start()
    for g in range(groups):
        own_q(g).start()
    for g in range(groups):
        own_do(g).start()
    plan_copy.start()
    seg_copy.start()

    for g in range(groups):
        for copy in own_kv(g):
            copy.wait()
        own_q(g).wait()
    pl.semaphore_wait(barrier, 3 + d + not_last.astype(jnp.int32) + not_first.astype(jnp.int32))
    signal(hello.at[0], up1)
    signal(hello.at[1], up2)

    @pl.when(d == 1)
    def _():
        signal(hello.at[2], across)


    def kv_copy(kind, g):
        source, place, target = (
            (4, 3 + 2 * d, other),
            (4, 2, up1),
            (4, 0, up2),
            (5 - 2 * d, 3 - 2 * d, up1),
            (5 - 2 * d, 1 + 4 * d, at(2 - 3 * d, d)),
        )[kind]
        return remote(
            kv.at[g, pl.ds(pl.multiple_of(source * rows, rows), rows)],
            kv.at[g, pl.ds(pl.multiple_of(place * rows, rows), rows)],
            kv_send.at[kind, g],
            kv_recv.at[kind, g],
            target,
        )

    def q_other(g):
        first, place = half * (2 - d), 3 * half * d
        return remote(
            qb.at[g, pl.ds(pl.multiple_of(first, half), half)],
            qb.at[g, pl.ds(pl.multiple_of(place, half), half)],
            q_send.at[0, g],
            q_recv.at[0, g],
            other,
        )

    def q_across(g):
        first, place = half * (1 + d), 3 * half * (1 - d)
        return remote(
            qb.at[g, pl.ds(pl.multiple_of(first, half), half)],
            qb.at[g, pl.ds(pl.multiple_of(place, half), half)],
            q_send.at[1, g],
            q_recv.at[1, g],
            across,
        )

    for g in range(groups):
        kv_copy(0, g).start()
    kv_copy(1, 0).start()
    kv_copy(2, 0).start()

    q_other(0).start()

    plan_copy.wait()
    seg_copy.wait()
    zeros = jnp.zeros((pad, 2 * HEAD_SIZE), F32)
    shifts = []
    row_at = lax.broadcasted_iota(jnp.int32, seg_ref.shape, 0)
    for s in range(2):
        block = plan_ref[2 * me + s]
        shifts.append(block - 2 * me + 1)
        pair = lax.div(block, 2)
        line = jnp.sum(jnp.where(row_at == pair, seg_ref[...].astype(F32), 0.0), axis=0, keepdims=True)
        lane = lax.broadcasted_iota(jnp.int32, (half, rows), 1)
        sub = lax.broadcasted_iota(jnp.int32, (half, rows), 0)
        picked = jnp.where(lane == sub + (block - 2 * pair) * half, jnp.broadcast_to(line, (half, rows)), 0.0)
        mine = jnp.sum(picked, axis=1, keepdims=True)

        def count(r, total, mine=mine):
            row = seg_ref[pl.ds(r, 1), :].astype(F32)
            return total + jnp.where(row < mine, 1.0, 0.0)

        total = lax.fori_loop(0, seg_ref.shape[0], count, jnp.zeros((half, rows), F32))
        first = jnp.sum(total, axis=1, keepdims=True)
        key_at = lax.broadcasted_iota(jnp.int32, (half, window), 1) + (block - 7) * half
        query_at = lax.broadcasted_iota(jnp.int32, (half, window), 0) + block * half
        seen = (key_at.astype(F32) >= first) & (key_at <= query_at)
        bias[s] = jnp.where(seen, 0.0, LOW)
        parts[s, pl.ds(0, pad)] = zeros
        parts[s, pl.ds(pad + window, pad + rows - half)] = jnp.zeros((pad + rows - half, 2 * HEAD_SIZE), F32)

    @pl.when(d == 0)
    def _():
        pl.semaphore_wait(hello.at[2], 1)

    q_across(0).start()
    for g in range(1, groups):
        q_other(g).start()
        q_across(g).start()
    pl.semaphore_wait(hello.at[0], 1)
    pl.semaphore_wait(hello.at[1], 1)

    def relay(g, carry):
        kv_copy(0, g).wait_recv()
        kv_copy(3, g).start()
        kv_copy(4, g).start()

        @pl.when(g + 1 < groups)
        def _():
            kv_copy(1, g + 1).start()
            kv_copy(2, g + 1).start()

        return carry

    lax.fori_loop(0, groups, relay, 0)
    for g in range(groups):
        own_do(g).wait()

    def columns(g):
        return pl.ds(pl.multiple_of(g * width, width), width)

    def att_copy(g):
        return remote(att.at[g], so_out.at[:, columns(g)], out_send.at[0, g], out_recv.at[0, g], later)

    def dq_copy(g):
        return remote(dqb.at[g], qg_out.at[:, columns(g)], out_send.at[1, g], out_recv.at[1, g], earlier)

    def ret_copy(g, kind):
        source, target = ((0, down2), (2, down1), (3 - 2 * d, down1), (1 + 4 * d, at(3 * d - 2, d)))[kind]
        return remote(ret.at[g, source], back.at[g, kind], ret_send.at[g, kind], ret_recv.at[g, kind], target)

    def fin_copy(g):
        return remote(psend.at[g], precv.at[g], fin_send.at[g], fin_recv.at[g], other)

    def window_part(o):
        total = None
        for s in range(2):
            starts = [pl.multiple_of(pad - k * half + o * rows, half) for k in range(4)]
            one = one_of(shifts[s], [parts[s, pl.ds(start, rows), :] for start in starts])
            total = one if total is None else total + one
        return total

    def pass_on(g):
        for kind in (3, 2):
            ret_copy(g, kind).wait_recv()
        total = loc[g, 1] + back[g, 2].astype(F32) + back[g, 3].astype(F32)
        psend[g] = total.astype(BF16)
        fin_copy(g).start()

    behind = (lax.rem(p, 4) == 1) | (lax.rem(p, 4) == 2)

    def one_group(g, carry):
        for kind in range(1, 5):
            kv_copy(kind, g).wait_recv()
        q_other(g).wait_recv()
        q_across(g).wait_recv()
        for s in range(2):
            shift = shifts[s]
            chosen = one_of(shift, [qb[g, pl.ds(k * half, half), :] for k in range(4)])
            grad = dob[g, pl.ds(s * half, half), :]
            heads = [slice(h * HEAD_SIZE, (h + 1) * HEAD_SIZE) for h in range(GROUP)]
            qs = jnp.concatenate([chosen[:, h] for h in heads], axis=0)
            gs = jnp.concatenate([grad[:, h] for h in heads], axis=0)
            ks = one_of(shift, [kv[g, pl.ds(k * half, window), pl.ds(0, HEAD_SIZE)] for k in range(4)])
            vs = one_of(shift, [kv[g, pl.ds(k * half, window), pl.ds(HEAD_SIZE, HEAD_SIZE)] for k in range(4)])
            scores = _nt(qs, ks).reshape(GROUP, half, window) + bias[s][None]
            scores = scores.reshape(GROUP * half, window)
            top = jnp.max(scores, axis=1, keepdims=True)
            weights = jnp.exp2((scores - top) * exp_scale)
            probs = weights * (1.0 / jnp.sum(weights, axis=1, keepdims=True))
            low = probs.astype(BF16)
            attended = _nn(low, vs).astype(BF16)
            grad_probs = _nt(gs, vs)
            delta = jnp.sum(gs.astype(F32) * attended.astype(F32), axis=1, keepdims=True)
            grad_scores = (probs * (grad_probs - delta)).astype(BF16)
            query_grad = (_nn(grad_scores, ks) * scale).astype(BF16)
            for h in range(GROUP):
                att[g, pl.ds(s * half, half), heads[h]] = attended[h * half : (h + 1) * half]
                dqb[g, pl.ds(s * half, half), heads[h]] = query_grad[h * half : (h + 1) * half]
            parts[s, pl.ds(pad, window), pl.ds(0, HEAD_SIZE)] = _tn(grad_scores, qs) * scale
            parts[s, pl.ds(pad, window), pl.ds(HEAD_SIZE, HEAD_SIZE)] = _tn(low, gs)
        for o in range(6):
            ret[g, o] = window_part(o).astype(BF16)
        loc[g, 0] = window_part(4)
        loc[g, 1] = window_part(5 - 2 * d)
        for kind in (3, 2, 0, 1):
            ret_copy(g, kind).start()

        @pl.when(not_last & ((g < groups - 1) | jnp.logical_not(behind)))
        def _():
            att_copy(g).start()

        @pl.when(not_first & ((g < groups - 1) | jnp.logical_not(behind)))
        def _():
            dq_copy(g).start()

        @pl.when(g > 0)
        def _():
            pass_on(g - 1)

        return carry

    lax.fori_loop(0, groups, one_group, 0)
    pass_on(groups - 1)

    @pl.when(not_last & behind)
    def _():
        att_copy(groups - 1).start()

    @pl.when(not_first & behind)
    def _():
        dq_copy(groups - 1).start()


    def finish(g, carry):
        for kind in (0, 1):
            ret_copy(g, kind).wait_recv()
        fin_copy(g).wait_recv()
        total = loc[g, 0] + back[g, 0].astype(F32) + back[g, 1].astype(F32) + precv[g].astype(F32)
        place = pl.ds(pl.multiple_of(g * HEAD_SIZE, HEAD_SIZE), HEAD_SIZE)
        kg_out[:, place] = total[:, :HEAD_SIZE].astype(BF16)
        vg_out[:, place] = total[:, HEAD_SIZE:].astype(BF16)
        return carry

    lax.fori_loop(0, groups, finish, 0)

    def drain(g, carry):
        for kind in range(5):
            kv_copy(kind, g).wait_send()
        q_other(g).wait_send()
        q_across(g).wait_send()
        for kind in range(4):
            ret_copy(g, kind).wait_send()
        fin_copy(g).wait_send()

        @pl.when(not_last)
        def _():
            att_copy(g).wait_send()
            dq_copy(g).wait_recv()

        @pl.when(not_first)
        def _():
            dq_copy(g).wait_send()
            att_copy(g).wait_recv()

        return carry

    lax.fori_loop(0, groups, drain, 0)


def _place(sizes, so_in, qg_in, kg_in, vg_in, so_out, qg_out, kg_out, vg_out, empty, sem):
    p = lax.axis_index("pipe")
    step = so_in.shape[0] // PIECES

    def pieces(source, to, first):
        return [
            pltpu.make_async_copy(source.at[pl.ds(k * step, step)], to.at[pl.ds(k * step, step)], sem.at[first + k])
            for k in range(PIECES)
        ]

    small = [
        pltpu.make_async_copy(kg_in, kg_out, sem.at[2 * PIECES]),
        pltpu.make_async_copy(vg_in, vg_out, sem.at[2 * PIECES + 1]),
    ]
    for source, to, first, none in ((so_in, so_out, 0, 0), (qg_in, qg_out, PIECES, sizes[0] - 1)):

        @pl.when(p != none)
        def _(source=source, to=to, first=first):
            for copy in pieces(source, to, first):
                copy.start()

        @pl.when(p == none)
        def _(to=to, first=first):
            empty[...] = jnp.zeros_like(empty)
            for copy in pieces(empty, to, first):
                copy.start()

    for copy in small:
        copy.start()
    for copy in pieces(so_in, so_out, 0) + pieces(qg_in, qg_out, PIECES) + small:
        copy.wait()


def _on_device(sizes, section_queries, section_keys, cascade_value_rows, output_grad, segments, stretch_plan):
    _, rows, width = section_queries.shape
    kv_width = section_keys.shape[2]
    groups, half = KEY_VALUE_HEADS, rows // 2
    share = width // groups
    hbm = pl.BlockSpec(memory_space=pltpu.HBM)
    vmem = pl.BlockSpec(memory_space=pltpu.VMEM)
    dma = pltpu.SemaphoreType.DMA
    attended, query_grad, key_grad, value_grad = pl.pallas_call(
        functools.partial(_kernel, sizes),
        out_shape=[
            pltpu.VMEM((rows, width), BF16),
            pltpu.VMEM((rows, width), BF16),
            pltpu.VMEM((rows, kv_width), BF16),
            pltpu.VMEM((rows, kv_width), BF16),
        ],
        in_specs=[hbm] * 6,
        out_specs=[vmem] * 4,
        scratch_shapes=[
            pltpu.SMEM(stretch_plan.shape, jnp.int32),
            pltpu.VMEM((segments.shape[0] // rows, rows), jnp.int32),
            pltpu.VMEM((groups, 6 * rows, 2 * HEAD_SIZE), BF16),
            pltpu.VMEM((groups, 2 * rows, share), BF16),
            pltpu.VMEM((groups, rows, share), BF16),
            pltpu.VMEM((groups, rows, share), BF16),
            pltpu.VMEM((groups, rows, share), BF16),
            pltpu.VMEM((2, half, 8 * half), F32),
            pltpu.VMEM((2, 14 * half + rows // 2, 2 * HEAD_SIZE), F32),
            pltpu.VMEM((groups, 2, rows, 2 * HEAD_SIZE), F32),
            pltpu.VMEM((groups, 6, rows, 2 * HEAD_SIZE), BF16),
            pltpu.VMEM((groups, 4, rows, 2 * HEAD_SIZE), BF16),
            pltpu.VMEM((groups, rows, 2 * HEAD_SIZE), BF16),
            pltpu.VMEM((groups, rows, 2 * HEAD_SIZE), BF16),
            dma((5, groups)),
            dma((5, groups)),
            dma((5, groups)),
            dma((2, groups)),
            dma((2, groups)),
            dma((2, groups)),
            dma((2, groups)),
            dma((groups, 4)),
            dma((groups, 4)),
            dma((groups,)),
            dma((groups,)),
            pltpu.SemaphoreType.REGULAR((3,)),
        ],
        compiler_params=pltpu.CompilerParams(
            collective_id=0, has_side_effects=True, vmem_limit_bytes=40 * 1024 * 1024
        ),
    )(
        *(
            pltpu.with_memory_space_constraint(value, pltpu.HBM)
            for value in (
                stretch_plan,
                segments.reshape(-1, rows),
                section_queries[0],
                section_keys[0],
                cascade_value_rows[0],
                output_grad[0],
            )
        )
    )
    section_output, query_grad_sent, key_grad, value_grad = pl.pallas_call(
        functools.partial(_place, sizes),
        out_shape=[
            jax.ShapeDtypeStruct((rows, width), BF16),
            jax.ShapeDtypeStruct((rows, width), BF16),
            jax.ShapeDtypeStruct((rows, kv_width), BF16),
            jax.ShapeDtypeStruct((rows, kv_width), BF16),
        ],
        in_specs=[vmem] * 4,
        out_specs=[hbm] * 4,
        scratch_shapes=[pltpu.VMEM((rows, width), BF16), dma((2 * PIECES + 2,))],
        compiler_params=pltpu.CompilerParams(vmem_limit_bytes=16 * 1024 * 1024),
    )(attended, query_grad, key_grad, value_grad)
    return section_output[None], query_grad_sent[None], key_grad[None], value_grad[None]


def solution(mesh):
    spread = P("pipe", ("ctx", "dp"), None)
    return jax.shard_map(
        functools.partial(_on_device, (mesh.shape["pipe"], mesh.shape["ctx"])),
        mesh=mesh,
        in_specs=(spread, spread, spread, spread, P(), P()),
        out_specs=(spread, spread, spread, spread),
        check_vma=False,
    )
```

```python
import functools
import math

import jax
import jax.numpy as jnp
from jax import lax
from jax.experimental import pallas as pl
from jax.experimental.pallas import tpu as pltpu
from jax.sharding import PartitionSpec as P

QUERY_HEADS = 32
KEY_VALUE_HEADS = 4
HEAD_SIZE = 128
GROUP = QUERY_HEADS // KEY_VALUE_HEADS
MESH = pl.DeviceIdType.MESH
F32 = jnp.float32
BF16 = jnp.bfloat16
LOW = -1e30
PIECES = 4


def _nt(a, b):
    return lax.dot_general(a, b, (((1,), (1,)), ((), ())), preferred_element_type=F32)


def _nn(a, b):
    return lax.dot_general(a, b, (((1,), (0,)), ((), ())), preferred_element_type=F32)


def _tn(a, b):
    return lax.dot_general(a, b, (((0,), (0,)), ((), ())), preferred_element_type=F32)


def one_of(index, choices):
    first, second, third, fourth = choices
    return lax.select(
        index < 2, lax.select(index == 0, first, second), lax.select(index == 2, third, fourth)
    )


def _kernel(
    sizes,
    plan_hbm,
    seg_hbm,
    q_hbm,
    k_hbm,
    v_hbm,
    do_hbm,
    so_out,
    qg_out,
    kg_out,
    vg_out,
    plan_ref,
    seg_ref,
    kv,
    qb,
    dob,
    att,
    dqb,
    bias,
    parts,
    loc,
    ret,
    back,
    psend,
    precv,
    loc_sem,
    kv_send,
    kv_recv,
    q_send,
    q_recv,
    out_send,
    out_recv,
    ret_send,
    ret_recv,
    fin_send,
    fin_recv,
    hello,
):
    n_pipe, n_ctx = sizes
    rows = k_hbm.shape[0]
    half = rows // 2
    width = GROUP * HEAD_SIZE
    window = 8 * half
    pad = 3 * half
    groups = KEY_VALUE_HEADS
    scale = 1.0 / math.sqrt(HEAD_SIZE)
    exp_scale = scale * math.log2(math.e)

    p = lax.axis_index("pipe")
    c = lax.axis_index("ctx")
    d = lax.axis_index("dp")
    me = 2 * c + d

    def at(dc, dd):
        return {"pipe": p, "ctx": lax.rem(c + dc + n_ctx, n_ctx), "dp": dd}

    other = at(0, 1 - d)
    across = at(2 * d - 1, 1 - d)
    up1, up2, down1, down2 = at(1, d), at(2, d), at(-1, d), at(-2, d)
    later = {"pipe": lax.rem(p + 1, n_pipe), "ctx": c, "dp": d}
    earlier = {"pipe": lax.rem(p + n_pipe - 1, n_pipe), "ctx": c, "dp": d}

    def remote(src, dst, send, recv, target):
        return pltpu.make_async_remote_copy(
            src_ref=src, dst_ref=dst, send_sem=send, recv_sem=recv, device_id=target, device_id_type=MESH
        )

    own = pl.ds(4 * rows, rows)

    def own_kv(g):
        part = pl.ds(pl.multiple_of(g * HEAD_SIZE, HEAD_SIZE), HEAD_SIZE)
        return (
            pltpu.make_async_copy(k_hbm.at[:, part], kv.at[g, own, pl.ds(0, HEAD_SIZE)], loc_sem.at[0, g]),
            pltpu.make_async_copy(v_hbm.at[:, part], kv.at[g, own, pl.ds(HEAD_SIZE, HEAD_SIZE)], loc_sem.at[1, g]),
        )

    def own_q(g):
        return pltpu.make_async_copy(
            q_hbm.at[:, pl.ds(pl.multiple_of(g * width, width), width)],
            qb.at[g, pl.ds(half, rows)],
            loc_sem.at[2, g],
        )

    def own_do(g):
        return pltpu.make_async_copy(
            do_hbm.at[:, pl.ds(pl.multiple_of(g * width, width), width)], dob.at[g], loc_sem.at[3, g]
        )

    barrier = pltpu.get_barrier_semaphore()
    not_first, not_last = p > 0, p < n_pipe - 1
    has_up1, has_up2, has_down1, has_down2 = c < n_ctx - 1, c < n_ctx - 2, c > 0, c > 1
    low, high = d == 0, d == 1
    side = (low & has_down1) | (high & has_up1)
    far_out = (low & has_up2) | (high & has_down1)
    far_in = (low & has_down2) | (high & has_up1)
    kv_out, kv_in = (None, has_up1, has_up2, has_up1, far_out), (None, has_down1, has_down2, has_down1, far_in)
    ret_out, ret_in = (has_down2, has_down1, has_down1, far_in), (has_up2, has_up1, has_up1, far_out)

    def when(condition, action):
        if condition is None:
            action()
        else:
            pl.when(condition)(action)

    def signal(semaphore, target):
        pl.semaphore_signal(semaphore, inc=1, device_id=target, device_id_type=MESH)

    signal(barrier, other)
    when(has_down1, lambda: signal(barrier, down1))
    when(has_down2, lambda: signal(barrier, down2))
    when(low & has_down1, lambda: signal(barrier, across))

    @pl.when(not_last)
    def _():
        signal(barrier, later)

    @pl.when(not_first)
    def _():
        signal(barrier, earlier)

    plan_copy = pltpu.make_async_copy(plan_hbm, plan_ref, loc_sem.at[4, 0])
    seg_copy = pltpu.make_async_copy(seg_hbm, seg_ref, loc_sem.at[4, 1])
    for g in range(groups):
        for copy in own_kv(g):
            copy.start()
    for g in range(groups):
        own_q(g).start()
    for g in range(groups):
        own_do(g).start()
    plan_copy.start()
    seg_copy.start()

    for g in range(groups):
        for copy in own_kv(g):
            copy.wait()
        own_q(g).wait()
    expected = 1
    for condition in (has_up1, has_up2, high & has_up1, not_last, not_first):
        expected = expected + condition.astype(jnp.int32)
    pl.semaphore_wait(barrier, expected)
    when(has_up1, lambda: signal(hello.at[0], up1))
    when(has_up2, lambda: signal(hello.at[1], up2))
    when(high & has_up1, lambda: signal(hello.at[2], across))


    def kv_copy(kind, g):
        source, place, target = (
            (4, 3 + 2 * d, other),
            (4, 2, up1),
            (4, 0, up2),
            (5 - 2 * d, 3 - 2 * d, up1),
            (5 - 2 * d, 1 + 4 * d, at(2 - 3 * d, d)),
        )[kind]
        return remote(
            kv.at[g, pl.ds(pl.multiple_of(source * rows, rows), rows)],
            kv.at[g, pl.ds(pl.multiple_of(place * rows, rows), rows)],
            kv_send.at[kind, g],
            kv_recv.at[kind, g],
            target,
        )

    def q_other(g):
        first, place = half * (2 - d), 3 * half * d
        return remote(
            qb.at[g, pl.ds(pl.multiple_of(first, half), half)],
            qb.at[g, pl.ds(pl.multiple_of(place, half), half)],
            q_send.at[0, g],
            q_recv.at[0, g],
            other,
        )

    def q_across(g):
        first, place = half * (1 + d), 3 * half * (1 - d)
        return remote(
            qb.at[g, pl.ds(pl.multiple_of(first, half), half)],
            qb.at[g, pl.ds(pl.multiple_of(place, half), half)],
            q_send.at[1, g],
            q_recv.at[1, g],
            across,
        )

    for g in range(groups):
        kv_copy(0, g).start()
    when(kv_out[1], lambda: kv_copy(1, 0).start())
    when(kv_out[2], lambda: kv_copy(2, 0).start())

    q_other(0).start()

    plan_copy.wait()
    seg_copy.wait()
    zeros = jnp.zeros((pad, 2 * HEAD_SIZE), F32)
    shifts = []
    row_at = lax.broadcasted_iota(jnp.int32, seg_ref.shape, 0)
    for s in range(2):
        block = plan_ref[2 * me + s]
        shifts.append(block - 2 * me + 1)
        pair = lax.div(block, 2)
        line = jnp.sum(jnp.where(row_at == pair, seg_ref[...].astype(F32), 0.0), axis=0, keepdims=True)
        lane = lax.broadcasted_iota(jnp.int32, (half, rows), 1)
        sub = lax.broadcasted_iota(jnp.int32, (half, rows), 0)
        picked = jnp.where(lane == sub + (block - 2 * pair) * half, jnp.broadcast_to(line, (half, rows)), 0.0)
        mine = jnp.sum(picked, axis=1, keepdims=True)

        def count(r, total, mine=mine):
            row = seg_ref[pl.ds(r, 1), :].astype(F32)
            return total + jnp.where(row < mine, 1.0, 0.0)

        total = lax.fori_loop(0, seg_ref.shape[0], count, jnp.zeros((half, rows), F32))
        first = jnp.sum(total, axis=1, keepdims=True)
        key_at = lax.broadcasted_iota(jnp.int32, (half, window), 1) + (block - 7) * half
        query_at = lax.broadcasted_iota(jnp.int32, (half, window), 0) + block * half
        seen = (key_at.astype(F32) >= first) & (key_at <= query_at)
        bias[s] = jnp.where(seen, 0.0, LOW)
        parts[s, pl.ds(0, pad)] = zeros
        parts[s, pl.ds(pad + window, pad + rows - half)] = jnp.zeros((pad + rows - half, 2 * HEAD_SIZE), F32)

    when(low & has_down1, lambda: pl.semaphore_wait(hello.at[2], 1))
    when(side, lambda: q_across(0).start())
    for g in range(1, groups):
        q_other(g).start()
        when(side, lambda g=g: q_across(g).start())
    when(has_down1, lambda: pl.semaphore_wait(hello.at[0], 1))
    when(has_down2, lambda: pl.semaphore_wait(hello.at[1], 1))

    def clear_rows(kind):
        place = (0, 2, 0, 3 - 2 * d, 1 + 4 * d)[kind]
        for g in range(groups):
            kv[g, pl.ds(pl.multiple_of(place * rows, rows), rows)] = jnp.zeros((rows, 2 * HEAD_SIZE), BF16)

    def clear_back(kind):
        for g in range(groups):
            back[g, kind] = jnp.zeros((rows, 2 * HEAD_SIZE), BF16)

    for kind in range(1, 5):
        when(jnp.logical_not(kv_in[kind]), lambda kind=kind: clear_rows(kind))
    for kind in range(4):
        when(jnp.logical_not(ret_in[kind]), lambda kind=kind: clear_back(kind))

    def relay(g, carry):
        kv_copy(0, g).wait_recv()
        when(kv_out[3], lambda: kv_copy(3, g).start())
        when(kv_out[4], lambda: kv_copy(4, g).start())
        when(kv_out[1] & (g + 1 < groups), lambda: kv_copy(1, g + 1).start())
        when(kv_out[2] & (g + 1 < groups), lambda: kv_copy(2, g + 1).start())

        return carry

    lax.fori_loop(0, groups, relay, 0)
    for g in range(groups):
        own_do(g).wait()

    def columns(g):
        return pl.ds(pl.multiple_of(g * width, width), width)

    def att_copy(g):
        return remote(att.at[g], so_out.at[:, columns(g)], out_send.at[0, g], out_recv.at[0, g], later)

    def dq_copy(g):
        return remote(dqb.at[g], qg_out.at[:, columns(g)], out_send.at[1, g], out_recv.at[1, g], earlier)

    def ret_copy(g, kind):
        source, target = ((0, down2), (2, down1), (3 - 2 * d, down1), (1 + 4 * d, at(3 * d - 2, d)))[kind]
        return remote(ret.at[g, source], back.at[g, kind], ret_send.at[g, kind], ret_recv.at[g, kind], target)

    def fin_copy(g):
        return remote(psend.at[g], precv.at[g], fin_send.at[g], fin_recv.at[g], other)

    def window_part(o):
        total = None
        for s in range(2):
            starts = [pl.multiple_of(pad - k * half + o * rows, half) for k in range(4)]
            one = one_of(shifts[s], [parts[s, pl.ds(start, rows), :] for start in starts])
            total = one if total is None else total + one
        return total

    def pass_on(g):
        for kind in (3, 2):
            when(ret_in[kind], lambda kind=kind: ret_copy(g, kind).wait_recv())
        total = loc[g, 1] + back[g, 2].astype(F32) + back[g, 3].astype(F32)
        psend[g] = total.astype(BF16)
        fin_copy(g).start()

    behind = (d == 1) & ((lax.rem(p, 4) == 1) | (lax.rem(p, 4) == 2))

    def one_group(g, carry):
        for kind in range(1, 5):
            when(kv_in[kind], lambda kind=kind: kv_copy(kind, g).wait_recv())
        q_other(g).wait_recv()
        when(side, lambda: q_across(g).wait_recv())
        for s in range(2):
            shift = shifts[s]
            chosen = one_of(shift, [qb[g, pl.ds(k * half, half), :] for k in range(4)])
            grad = dob[g, pl.ds(s * half, half), :]
            heads = [slice(h * HEAD_SIZE, (h + 1) * HEAD_SIZE) for h in range(GROUP)]
            qs = jnp.concatenate([chosen[:, h] for h in heads], axis=0)
            gs = jnp.concatenate([grad[:, h] for h in heads], axis=0)
            ks = one_of(shift, [kv[g, pl.ds(k * half, window), pl.ds(0, HEAD_SIZE)] for k in range(4)])
            vs = one_of(shift, [kv[g, pl.ds(k * half, window), pl.ds(HEAD_SIZE, HEAD_SIZE)] for k in range(4)])
            scores = _nt(qs, ks).reshape(GROUP, half, window) + bias[s][None]
            scores = scores.reshape(GROUP * half, window)
            top = jnp.max(scores, axis=1, keepdims=True)
            weights = jnp.exp2((scores - top) * exp_scale)
            probs = weights * (1.0 / jnp.sum(weights, axis=1, keepdims=True))
            low = probs.astype(BF16)
            attended = _nn(low, vs).astype(BF16)
            grad_probs = _nt(gs, vs)
            delta = jnp.sum(gs.astype(F32) * attended.astype(F32), axis=1, keepdims=True)
            grad_scores = (probs * (grad_probs - delta)).astype(BF16)
            query_grad = (_nn(grad_scores, ks) * scale).astype(BF16)
            for h in range(GROUP):
                att[g, pl.ds(s * half, half), heads[h]] = attended[h * half : (h + 1) * half]
                dqb[g, pl.ds(s * half, half), heads[h]] = query_grad[h * half : (h + 1) * half]
            parts[s, pl.ds(pad, window), pl.ds(0, HEAD_SIZE)] = _tn(grad_scores, qs) * scale
            parts[s, pl.ds(pad, window), pl.ds(HEAD_SIZE, HEAD_SIZE)] = _tn(low, gs)
        for o in range(6):
            ret[g, o] = window_part(o).astype(BF16)
        loc[g, 0] = window_part(4)
        loc[g, 1] = window_part(5 - 2 * d)
        for kind in (3, 2, 0, 1):
            when(ret_out[kind], lambda kind=kind: ret_copy(g, kind).start())

        @pl.when(not_last & ((g < groups - 1) | jnp.logical_not(behind)))
        def _():
            att_copy(g).start()

        @pl.when(not_first & ((g < groups - 1) | jnp.logical_not(behind)))
        def _():
            dq_copy(g).start()

        @pl.when(g > 0)
        def _():
            pass_on(g - 1)

        return carry

    lax.fori_loop(0, groups, one_group, 0)
    pass_on(groups - 1)

    @pl.when(not_last & behind)
    def _():
        att_copy(groups - 1).start()

    @pl.when(not_first & behind)
    def _():
        dq_copy(groups - 1).start()


    def finish(g, carry):
        for kind in (0, 1):
            when(ret_in[kind], lambda kind=kind: ret_copy(g, kind).wait_recv())
        fin_copy(g).wait_recv()
        total = loc[g, 0] + back[g, 0].astype(F32) + back[g, 1].astype(F32) + precv[g].astype(F32)
        place = pl.ds(pl.multiple_of(g * HEAD_SIZE, HEAD_SIZE), HEAD_SIZE)
        kg_out[:, place] = total[:, :HEAD_SIZE].astype(BF16)
        vg_out[:, place] = total[:, HEAD_SIZE:].astype(BF16)
        return carry

    lax.fori_loop(0, groups, finish, 0)

    def drain(g, carry):
        for kind in range(5):
            when(kv_out[kind], lambda kind=kind: kv_copy(kind, g).wait_send())
        q_other(g).wait_send()
        when(side, lambda: q_across(g).wait_send())
        for kind in range(4):
            when(ret_out[kind], lambda kind=kind: ret_copy(g, kind).wait_send())
        fin_copy(g).wait_send()

        @pl.when(not_last)
        def _():
            att_copy(g).wait_send()
            dq_copy(g).wait_recv()

        @pl.when(not_first)
        def _():
            dq_copy(g).wait_send()
            att_copy(g).wait_recv()

        return carry

    lax.fori_loop(0, groups, drain, 0)


def _place(sizes, so_in, qg_in, kg_in, vg_in, so_out, qg_out, kg_out, vg_out, empty, sem):
    p = lax.axis_index("pipe")
    step = so_in.shape[0] // PIECES

    def pieces(source, to, first):
        return [
            pltpu.make_async_copy(source.at[pl.ds(k * step, step)], to.at[pl.ds(k * step, step)], sem.at[first + k])
            for k in range(PIECES)
        ]

    small = [
        pltpu.make_async_copy(kg_in, kg_out, sem.at[2 * PIECES]),
        pltpu.make_async_copy(vg_in, vg_out, sem.at[2 * PIECES + 1]),
    ]
    for source, to, first, none in ((so_in, so_out, 0, 0), (qg_in, qg_out, PIECES, sizes[0] - 1)):

        @pl.when(p != none)
        def _(source=source, to=to, first=first):
            for copy in pieces(source, to, first):
                copy.start()

        @pl.when(p == none)
        def _(to=to, first=first):
            empty[...] = jnp.zeros_like(empty)
            for copy in pieces(empty, to, first):
                copy.start()

    for copy in small:
        copy.start()
    for copy in pieces(so_in, so_out, 0) + pieces(qg_in, qg_out, PIECES) + small:
        copy.wait()


def _on_device(sizes, section_queries, section_keys, cascade_value_rows, output_grad, segments, stretch_plan):
    _, rows, width = section_queries.shape
    kv_width = section_keys.shape[2]
    groups, half = KEY_VALUE_HEADS, rows // 2
    share = width // groups
    hbm = pl.BlockSpec(memory_space=pltpu.HBM)
    vmem = pl.BlockSpec(memory_space=pltpu.VMEM)
    dma = pltpu.SemaphoreType.DMA
    attended, query_grad, key_grad, value_grad = pl.pallas_call(
        functools.partial(_kernel, sizes),
        out_shape=[
            pltpu.VMEM((rows, width), BF16),
            pltpu.VMEM((rows, width), BF16),
            pltpu.VMEM((rows, kv_width), BF16),
            pltpu.VMEM((rows, kv_width), BF16),
        ],
        in_specs=[hbm] * 6,
        out_specs=[vmem] * 4,
        scratch_shapes=[
            pltpu.SMEM(stretch_plan.shape, jnp.int32),
            pltpu.VMEM((segments.shape[0] // rows, rows), jnp.int32),
            pltpu.VMEM((groups, 6 * rows, 2 * HEAD_SIZE), BF16),
            pltpu.VMEM((groups, 2 * rows, share), BF16),
            pltpu.VMEM((groups, rows, share), BF16),
            pltpu.VMEM((groups, rows, share), BF16),
            pltpu.VMEM((groups, rows, share), BF16),
            pltpu.VMEM((2, half, 8 * half), F32),
            pltpu.VMEM((2, 14 * half + rows // 2, 2 * HEAD_SIZE), F32),
            pltpu.VMEM((groups, 2, rows, 2 * HEAD_SIZE), F32),
            pltpu.VMEM((groups, 6, rows, 2 * HEAD_SIZE), BF16),
            pltpu.VMEM((groups, 4, rows, 2 * HEAD_SIZE), BF16),
            pltpu.VMEM((groups, rows, 2 * HEAD_SIZE), BF16),
            pltpu.VMEM((groups, rows, 2 * HEAD_SIZE), BF16),
            dma((5, groups)),
            dma((5, groups)),
            dma((5, groups)),
            dma((2, groups)),
            dma((2, groups)),
            dma((2, groups)),
            dma((2, groups)),
            dma((groups, 4)),
            dma((groups, 4)),
            dma((groups,)),
            dma((groups,)),
            pltpu.SemaphoreType.REGULAR((3,)),
        ],
        compiler_params=pltpu.CompilerParams(
            collective_id=0, has_side_effects=True, vmem_limit_bytes=40 * 1024 * 1024
        ),
    )(
        *(
            pltpu.with_memory_space_constraint(value, pltpu.HBM)
            for value in (
                stretch_plan,
                segments.reshape(-1, rows),
                section_queries[0],
                section_keys[0],
                cascade_value_rows[0],
                output_grad[0],
            )
        )
    )
    section_output, query_grad_sent, key_grad, value_grad = pl.pallas_call(
        functools.partial(_place, sizes),
        out_shape=[
            jax.ShapeDtypeStruct((rows, width), BF16),
            jax.ShapeDtypeStruct((rows, width), BF16),
            jax.ShapeDtypeStruct((rows, kv_width), BF16),
            jax.ShapeDtypeStruct((rows, kv_width), BF16),
        ],
        in_specs=[vmem] * 4,
        out_specs=[hbm] * 4,
        scratch_shapes=[pltpu.VMEM((rows, width), BF16), dma((2 * PIECES + 2,))],
        compiler_params=pltpu.CompilerParams(vmem_limit_bytes=16 * 1024 * 1024),
    )(attended, query_grad, key_grad, value_grad)
    return section_output[None], query_grad_sent[None], key_grad[None], value_grad[None]


def solution(mesh):
    spread = P("pipe", ("ctx", "dp"), None)
    return jax.shard_map(
        functools.partial(_on_device, (mesh.shape["pipe"], mesh.shape["ctx"])),
        mesh=mesh,
        in_specs=(spread, spread, spread, spread, P(), P()),
        out_specs=(spread, spread, spread, spread),
        check_vma=False,
    )
```
